256 devices in a mesh: row: 8 (over y_lo, x), col: 32 (over z, y_hi, core).
Axes of the slice: x: 4, y: 4 (y_hi: 2, y_lo: 2; y = y_hi * 2 + y_lo), z: 8, core: 2. Of those that a mesh axis runs over, the one named last changes fastest.
Arguments:
- left_features: bfloat16 [32, 2048, 320], P('row', 'col'), may hold values from -6 to 6
- right_features: bfloat16 [32, 2048, 320], P('row', 'col'), may hold values from -6 to 6
- conv_weight: bfloat16 [3, 3, 3, 40, 32], replicated, may hold values from -0.1875 to 0.1875
- cotangent: bfloat16 [24, 32, 2048, 32], P(None, 'row', 'col'), may hold values from -6 to 6
Outputs:
- cost_output: bfloat16 [24, 32, 2048, 32], P(None, 'row', 'col')
- weight_grad: float32 [3, 3, 3, 40, 32], replicated
- left_grad: bfloat16 [32, 2048, 320], P('row', 'col')
- right_grad: bfloat16 [32, 2048, 320], P('row', 'col')
The draws below stay inside these ranges and needn't reach their ends.
All inputs are finite; a program needn't handle non-finite values.
Results may differ from the reference program's by a relative error of at most 0.0049.
Values may be sent and summed in bfloat16 or wider, within the bound.
A program may use at most 128 MiB of HBM per device.

```python
import math
import jax
import jax.numpy as jnp
from jax import lax

C = 320
G = 40
F = 32
DISP = 24
STEP = 4
H = 32
W = 2048


def shard_levels(key, extent, pieces, smallest, top_value):
    def one(dim, shards_of):
        draws = jax.random.uniform(jax.random.fold_in(jax.random.fold_in(key, 6), dim), (shards_of,), jnp.float32, smallest / len(pieces), top_value / len(pieces))
        return jnp.repeat(jnp.exp(draws), extent[dim] // shards_of).reshape((-1,) + (1,) * (len(extent) - dim - 1))

    loudness = one(*pieces[0])
    for cut in pieces[1:]:
        loudness = loudness * one(*cut)
    return loudness


def noise(key, extent, deviation, reach, cuts=(), held_as=jnp.bfloat16):
    gain = shard_levels(key, extent, cuts, -0.22, 0.18) if cuts else 1.0
    result = jax.random.normal(key, extent, jnp.float32) * deviation * gain
    return jnp.minimum(jnp.maximum(result, -reach), reach).astype(held_as)


def setup_inputs(seed: int = 0) -> dict:
    arg_keys = jax.random.split(jax.random.key(seed), 5)
    return {
        "left_features": noise(arg_keys[0], (H, W, C), 1.0, 6.0, ((0, 8), (1, 32))),
        "right_features": noise(arg_keys[1], (H, W, C), 1.0, 6.0, ((0, 8), (1, 32))),
        "conv_weight": noise(arg_keys[2], (3, 3, 3, G, F), (27 * G) ** -0.5, 0.1875),
        "cotangent": noise(arg_keys[3], (DISP, H, W, F), 1.0, 6.0, ((1, 8), (2, 32))),
    }


DIMS = ('NDHWC', 'DHWIO', 'NDHWC')

def conv_volume(volume, kernel):
    return lax.conv_general_dilated(volume[None], kernel, (1, 1, 1), ((1, 1), (1, 1), (1, 1)), dimension_numbers=DIMS, precision=lax.Precision.HIGHEST)[0]

def reference(left_features, right_features, conv_weight, cotangent):
    image_height, image_width, channels = left_features.shape
    groups = conv_weight.shape[3]
    group_size = channels // groups
    left_f = left_features.astype(jnp.float32).reshape(image_height, image_width, groups, group_size)
    right_f = right_features.astype(jnp.float32)
    planes = []
    for disp_index in range(DISP):
        offset = STEP * disp_index
        shifted = jnp.pad(right_f, ((0, 0), (offset, 0), (0, 0)))[:, :image_width]
        shifted = shifted.reshape(image_height, image_width, groups, group_size)
        planes.append(lax.optimization_barrier(jnp.sum(left_f * shifted, axis=3)) / group_size)
    volume = lax.optimization_barrier(jnp.stack(planes).astype(jnp.bfloat16)).astype(jnp.float32)
    output, pullback = jax.vjp(conv_volume, volume, conv_weight.astype(jnp.float32))
    grad_volume, grad_kernel = pullback(cotangent.astype(jnp.float32))
    grad_volume = lax.optimization_barrier(grad_volume.astype(jnp.bfloat16)).astype(jnp.float32)
    weight_grad = grad_kernel / math.sqrt(DISP * image_height * image_width)
    left_accum = jnp.zeros((image_height, image_width, groups, group_size), jnp.float32)
    right_accum = jnp.zeros((image_height, image_width, channels), jnp.float32)
    for disp_index in range(DISP):
        offset = STEP * disp_index
        shifted = jnp.pad(right_f, ((0, 0), (offset, 0), (0, 0)))[:, :image_width]
        shifted = shifted.reshape(image_height, image_width, groups, group_size)
        left_accum = left_accum + grad_volume[disp_index][..., None] * shifted
        contrib = (grad_volume[disp_index][..., None] * left_f).reshape(image_height, image_width, channels)
        right_accum = right_accum + jnp.pad(contrib, ((0, 0), (0, offset), (0, 0)))[:, offset:]
    left_grad = (left_accum / group_size).reshape(image_height, image_width, channels).astype(jnp.bfloat16)
    right_grad = (right_accum / group_size).astype(jnp.bfloat16)
    return (output.astype(jnp.bfloat16), weight_grad, left_grad, right_grad)
```

```python
import functools
import math

import jax
import jax.numpy as jnp
from jax import lax
from jax.experimental import pallas as pl
from jax.experimental.pallas import tpu as pltpu
from jax.sharding import PartitionSpec as P

DISP = 24
STEP = 4
OUT_D = 6
IN_D = OUT_D + 2
WINDOWS = DISP // OUT_D
LANES = 256
BF = jnp.bfloat16
F32 = jnp.float32
MESH = pl.DeviceIdType.MESH
NEIGHBOURS = [(dr, dc) for dr in (-1, 0, 1) for dc in (-1, 0, 1) if (dr, dc) != (0, 0)]


def dot(a, b, contract=((1,), (0,))):
    return lax.dot_general(a, b, (contract, ((), ())), preferred_element_type=F32)


def iota(shape, dim):
    return lax.broadcasted_iota(jnp.int32, shape, dim)


def kernel(
    nrow, ncol, chunk, owners, scale,
    l_ref, r_ref, w_ref, c_ref,
    cost_ref, wg_ref, lg_ref, rg_ref,
    rband, rf0, rf4, lf, sel, band_n, band_t, cs, vs, vt, edge_c, edge_v, halo_c, halo_v,
    gv, spread, racc0, racc4, back_send, back_recv, dsum, slots1, part2, slots2, full, obuf,
    sem_rs, sem_rr, sem_cs, sem_cr, sem_vs, sem_vr, sem_bs, sem_br,
    sem1_s, sem1_r, sem2_s, sem2_r, sem3_s, sem3_r,
):
    rows, cols, channels = l_ref.shape
    groups, feats = w_ref.shape[3], w_ref.shape[4]
    group_size = channels // groups
    cells = rows * cols
    row, col = lax.axis_index("row"), lax.axis_index("col")

    def at(dr, dc):
        return (lax.rem(row + dr + nrow, nrow), lax.rem(col + dc + ncol, ncol))

    barrier = pltpu.get_barrier_semaphore()

    def hello_col(step, carry):
        pl.semaphore_signal(barrier, inc=1, device_id=at(0, step), device_id_type=MESH)
        return carry

    def hello_row(step, carry):
        pl.semaphore_signal(barrier, inc=1, device_id=at(step, 0), device_id_type=MESH)
        return carry

    lax.fori_loop(1, ncol, hello_col, 0)
    lax.fori_loop(1, nrow, hello_row, 0)
    for dr, dc in NEIGHBOURS:
        if dr != 0 and dc != 0:
            pl.semaphore_signal(barrier, inc=1, device_id=at(dr, dc), device_id_type=MESH)
    pl.semaphore_wait(barrier, ncol - 1 + nrow - 1 + 4)

    def copy(src, dst, send, recv, target):
        return pltpu.make_async_remote_copy(
            src_ref=src, dst_ref=dst, send_sem=send, recv_sem=recv,
            device_id=target, device_id_type=MESH,
        )

    right_copies = [
        copy(r_ref, rband.at[:, 32:96], sem_rs.at[0], sem_rr.at[0], at(0, 1)),
        copy(r_ref.at[:, cols - 32 : cols], rband.at[:, 0:32], sem_rs.at[1], sem_rr.at[1], at(0, 2)),
    ]
    for c in right_copies:
        c.start()

    def halo_copies(body, edge, halo, send, recv):
        out = []
        for n, (dr, dc) in enumerate(NEIGHBOURS):
            if dc == 0:
                src = body.at[1, :, rows if dr == 1 else 1]
                dst = body.at[1, :, 0 if dr == 1 else rows + 1]
            else:
                src = edge.at[1 if dc == 1 else 0]
                dst = halo.at[0 if dc == 1 else 1, 1 - dr]
            out.append(copy(src, dst, send.at[n], recv.at[n], at(dr, dc)))
        return out

    def edge_pieces(body):
        first, last = [], []
        for k in range(WINDOWS):
            for h in range(rows):
                first.append(body[1, k, 1 + h, 0:16].astype(F32)[0:1])
                last.append(body[1, k, 1 + h, cols - 16 : cols].astype(F32)[15:16])
        return first, last

    def fill_edges(edge, body):
        for side, lines in enumerate(edge_pieces(body)):
            acc = jnp.zeros((16, LANES), F32)
            for n, line in enumerate(lines):
                acc = jnp.where(iota((16, LANES), 0) == n, line, acc)
            edge[side] = acc.astype(BF)

    def clear_outside(body, halo):
        for cond, u, h in ((row == 0, 0, 0), (row == nrow - 1, 2, rows + 1)):
            @pl.when(cond)
            def _():
                for k in range(WINDOWS):
                    body[1, k, h] = jnp.zeros((cols, LANES), BF)
                for side in range(2):
                    halo[side, u] = jnp.zeros((16, LANES), BF)
        for cond, side in ((col == 0, 0), (col == ncol - 1, 1)):
            @pl.when(cond)
            def _():
                for u in range(3):
                    halo[side, u] = jnp.zeros((16, LANES), BF)

    def write_shifts(body, halo):
        lines = [[halo[side, u].astype(F32) for u in range(3)] for side in range(2)]
        where = iota((cols, LANES), 0)
        for k in range(WINDOWS):
            for h in range(rows + 2):
                u, n = (0, rows - 1) if h == 0 else ((2, 0) if h == rows + 1 else (1, h - 1))
                n = n + rows * k
                mid = body[1, k, h].astype(F32)
                before = jnp.where(where == 0, lines[0][u][n : n + 1], pltpu.roll(mid, 1, 0))
                after = jnp.where(where == cols - 1, lines[1][u][n : n + 1], pltpu.roll(mid, cols - 1, 0))
                body[0, k, h] = before.astype(BF)
                body[2, k, h] = after.astype(BF)

    for k in range(WINDOWS):
        parts = []
        for j in range(IN_D):
            d = OUT_D * k - 1 + j
            if 0 <= d < DISP:
                parts.append(c_ref[d].reshape(cells, feats))
            else:
                parts.append(jnp.zeros((cells, feats), BF))
        cs[1, k, 1 : rows + 1] = jnp.concatenate(parts, axis=1).reshape(rows, cols, LANES)
    fill_edges(edge_c, cs)
    cot_copies = halo_copies(cs, edge_c, halo_c, sem_cs, sem_cr)
    for c in cot_copies:
        c.start()

    lf[...] = l_ref[...].astype(F32)
    for i in range(OUT_D):
        r = iota((channels, LANES), 0) + i * channels
        sel[i] = jnp.where(r // group_size == iota((channels, LANES), 1), 1.0, 0.0).astype(BF)
    f_idx = iota((feats, OUT_D * LANES), 0)
    lane = iota((feats, OUT_D * LANES), 1)
    banded = jnp.zeros((9 * groups, OUT_D * LANES), F32)
    for a in range(3):
        tap = jnp.where(
            (lane % feats == f_idx) & (lane // LANES - (lane % LANES) // feats + 2 == a), 1.0, 0.0
        ).astype(BF)
        wa = w_ref[a].astype(F32).reshape(9 * groups, feats).astype(BF)
        banded = banded + dot(wa, tap)
    for n in range(9):
        tall = [banded[groups * n : groups * (n + 1), LANES * i : LANES * (i + 1)] for i in range(OUT_D)]
        tall.append(jnp.zeros((LANES - OUT_D * groups, LANES), F32))
        tall = jnp.concatenate(tall, axis=0)
        band_n[LANES * n : LANES * (n + 1)] = tall.astype(BF)
        band_t[LANES * n : LANES * (n + 1)] = tall.T.astype(BF)

    for c in right_copies:
        c.wait_recv()
    @pl.when(col < 1)
    def _():
        rband[:, 32:96] = jnp.zeros((rows, 64, channels), BF)

    @pl.when(col < 2)
    def _():
        rband[:, 0:32] = jnp.zeros((rows, 32, channels), BF)

    for h in range(rows):
        rf0[h, 0:96] = rband[h].astype(F32)
        rf0[h, 96:160] = r_ref[h].astype(F32)
        rf4[h, 0:152] = rf0[h, 4:156]
        rf4[h, 152:160] = rf0[h, 152:160]

    def shifted(k, i, h=None):
        start = pl.multiple_of(96 - STEP * (OUT_D * k + i) - (STEP if i % 2 else 0), 8)
        src = rf4 if i % 2 else rf0
        if h is None:
            return src[:, pl.ds(start, cols)]
        return src[h, pl.ds(start, cols)]

    def volume(k, carry):
        acc = jnp.zeros((cells, LANES), F32)
        for i in range(OUT_D):
            product = (lf[...] * shifted(k, i)).astype(BF).reshape(cells, channels)
            acc = acc + dot(product, sel[i])
        acc = (acc * (1.0 / group_size)).astype(BF)
        vs[1, k, 1 : rows + 1] = acc.reshape(rows, cols, LANES)
        vt[k] = acc.T
        return carry

    lax.fori_loop(0, WINDOWS, volume, 0)
    fill_edges(edge_v, vs)
    vol_copies = halo_copies(vs, edge_v, halo_v, sem_vs, sem_vr)
    for c in vol_copies:
        c.start()

    for c in cot_copies:
        c.wait_recv()
    clear_outside(cs, halo_c)
    write_shifts(cs, halo_c)

    dsum[9 * groups :] = jnp.zeros((dsum.shape[0] - 9 * groups, 128), F32)

    def kernel_grad(n, carry):
        t, hb = 2 - n % 3, 2 - n // 3
        acc = jnp.zeros((LANES, LANES), F32)
        for k in range(WINDOWS):
            acc = acc + dot(vt[k], cs[t, k, pl.ds(hb, rows)].reshape(cells, LANES))
        total = acc[0:groups]
        for i in range(1, OUT_D):
            total = total + pltpu.roll(acc[groups * i : groups * (i + 1)], LANES - feats * i, 1)
        dsum[pl.ds(pl.multiple_of(n * groups, 8), groups)] = total[:, 0:128]
        return carry

    lax.fori_loop(0, 9, kernel_grad, 0)

    own_rows = pl.ds(pl.multiple_of(col * chunk, 8), chunk)

    def send1(step, carry):
        r, c = at(0, step)

        @pl.when(c < owners)
        def _():
            copy(
                dsum.at[pl.ds(pl.multiple_of(c * chunk, 8), chunk)], slots1.at[col],
                sem1_s.at[step], sem1_r.at[col], (r, c),
            ).start()
        return carry

    lax.fori_loop(1, ncol, send1, 0)

    def grad_volume(k, carry):
        taps = []
        for b in range(3):
            for e in range(3):
                taps.append(cs[2 - e, k, 2 - b : 2 - b + rows].reshape(cells, LANES))
        gv[k] = dot(jnp.concatenate(taps, axis=1), band_t[...]).astype(BF)
        return carry

    lax.fori_loop(0, WINDOWS, grad_volume, 0)

    @pl.when(col < owners)
    def _():
        slots1[col] = dsum[own_rows]

        def wait1(step, carry):
            _, c = at(0, step)
            copy(slots1.at[c], slots1.at[c], sem1_s.at[step], sem1_r.at[c], at(0, step)).wait_recv()
            return carry

        lax.fori_loop(1, ncol, wait1, 0)
        total = slots1[0]
        for q in range(1, ncol):
            total = total + slots1[q]
        part2[...] = total
        slots2[row] = total

        def send2(step, carry):
            copy(part2, slots2.at[row], sem2_s.at[step], sem2_r.at[row], at(step, 0)).start()
            return carry

        lax.fori_loop(1, nrow, send2, 0)

    racc0[...] = jnp.zeros_like(racc0)
    racc4[...] = jnp.zeros_like(racc4)
    lacc = spread.at[0]
    lacc[...] = jnp.zeros((cells, channels), F32)

    def feature_grads(k, carry):
        for i in range(OUT_D):
            spread[1] = dot(gv[k], sel[i], ((1,), (1,)))
            start = pl.multiple_of(96 - STEP * (OUT_D * k + i) - (STEP if i % 2 else 0), 8)
            acc = racc4 if i % 2 else racc0
            for h in range(rows):
                s = spread[1, cols * h : cols * (h + 1)]
                lacc[cols * h : cols * (h + 1)] += s * shifted(k, i, h)
                acc[h, pl.ds(start, cols)] += s * lf[h]
        return carry

    lax.fori_loop(0, WINDOWS, feature_grads, 0)
    inv = 1.0 / group_size
    lg_ref[...] = (lacc[...] * inv).reshape(rows, cols, channels).astype(BF)
    for h in range(rows):
        racc0[h, 4:156] += racc4[h, 0:152]
        back_send[h] = racc0[h, 0:96].astype(BF)
    back_copies = [
        copy(back_send.at[:, 32:96], back_recv.at[:, 0:64], sem_bs.at[0], sem_br.at[0], at(0, -1)),
        copy(back_send.at[:, 0:32], back_recv.at[:, 64:96], sem_bs.at[1], sem_br.at[1], at(0, -2)),
    ]
    for c in back_copies:
        c.start()

    @pl.when(col < owners)
    def _():
        def wait2(step, carry):
            r, _ = at(step, 0)
            copy(part2, slots2.at[r], sem2_s.at[step], sem2_r.at[r], at(step, 0)).wait_recv()
            return carry

        lax.fori_loop(1, nrow, wait2, 0)
        total = slots2[0]
        for q in range(1, nrow):
            total = total + slots2[q]
        full[own_rows] = total * scale

        def send3(step, carry):
            copy(full.at[own_rows], full.at[own_rows], sem3_s.at[step], sem3_r.at[col], at(0, step)).start()
            return carry

        lax.fori_loop(1, ncol, send3, 0)

    for c in vol_copies:
        c.wait_recv()
    clear_outside(vs, halo_v)
    write_shifts(vs, halo_v)

    def forward(k, carry):
        taps = []
        for b in range(3):
            for e in range(3):
                taps.append(vs[e, k, b : b + rows].reshape(cells, LANES))
        obuf[k] = dot(jnp.concatenate(taps, axis=1), band_n[...])
        return carry

    lax.fori_loop(0, WINDOWS, forward, 0)
    for k in range(WINDOWS):
        for i in range(OUT_D):
            j = i + 1
            value = obuf[k, :, feats * j : feats * (j + 1)]
            if i == 0 and k > 0:
                value = value + obuf[k - 1, :, feats * (IN_D - 1) : feats * IN_D]
            if i == OUT_D - 1 and k < WINDOWS - 1:
                value = value + obuf[k + 1, :, 0:feats]
            cost_ref[OUT_D * k + i] = value.astype(BF).reshape(rows, cols, feats)

    for c in back_copies:
        c.wait_recv()
    near = jnp.where(col < ncol - 1, 1.0, 0.0).astype(F32)
    far = jnp.where(col < ncol - 2, 1.0, 0.0).astype(F32)
    for h in range(rows):
        own = racc0[h, 96:160] + near * back_recv[h, 0:64].astype(F32)
        tail = own[32:64] + far * back_recv[h, 64:96].astype(F32)
        rg_ref[h, 0:32] = (own[0:32] * inv).astype(BF)
        rg_ref[h, 32:64] = (tail * inv).astype(BF)

    def wait3(step, carry):
        _, c = at(0, step)

        @pl.when(c < owners)
        def _():
            piece = full.at[pl.ds(pl.multiple_of(c * chunk, 8), chunk)]
            copy(piece, piece, sem3_s.at[step], sem3_r.at[c], at(0, step)).wait_recv()
        return carry

    lax.fori_loop(1, ncol, wait3, 0)
    for b in range(3):
        for e in range(3):
            block = full[groups * (3 * b + e) : groups * (3 * b + e + 1)]
            for a in range(3):
                wg_ref[a, b, e] = block[:, feats * (2 - a) : feats * (3 - a)]

    for c in right_copies + cot_copies + vol_copies + back_copies:
        c.wait_send()

    def sent1(step, carry):
        _, c = at(0, step)

        @pl.when(c < owners)
        def _():
            copy(dsum.at[own_rows], slots1.at[col], sem1_s.at[step], sem1_r.at[col], at(0, step)).wait_send()
        return carry

    lax.fori_loop(1, ncol, sent1, 0)

    @pl.when(col < owners)
    def _():
        def sent2(step, carry):
            copy(part2, slots2.at[row], sem2_s.at[step], sem2_r.at[row], at(step, 0)).wait_send()
            return carry

        lax.fori_loop(1, nrow, sent2, 0)

        def sent3(step, carry):
            copy(full.at[own_rows], full.at[own_rows], sem3_s.at[step], sem3_r.at[col], at(0, step)).wait_send()
            return carry

        lax.fori_loop(1, ncol, sent3, 0)


def on_device(nrow, ncol, left, right, weight, cotangent):
    rows, cols, channels = left.shape
    groups, feats = weight.shape[3], weight.shape[4]
    cells = rows * cols
    chunk = -(-9 * groups // ncol)
    chunk = -(-chunk // 16) * 16
    owners = -(-9 * groups // chunk)
    scale = 1.0 / math.sqrt(DISP * rows * nrow * cols * ncol)
    dma = pltpu.SemaphoreType.DMA
    body = pltpu.VMEM((3, WINDOWS, rows + 2, cols, LANES), BF)
    edge = pltpu.VMEM((2, 16, LANES), BF)
    halo = pltpu.VMEM((2, 3, 16, LANES), BF)
    scratch = [
        pltpu.VMEM((rows, 96, channels), BF),
        pltpu.VMEM((rows, 160, channels), F32),
        pltpu.VMEM((rows, 160, channels), F32),
        pltpu.VMEM((rows, cols, channels), F32),
        pltpu.VMEM((OUT_D, channels, LANES), BF),
        pltpu.VMEM((9 * LANES, LANES), BF),
        pltpu.VMEM((9 * LANES, LANES), BF),
        body, body,
        pltpu.VMEM((WINDOWS, LANES, cells), BF),
        edge, edge, halo, halo,
        pltpu.VMEM((WINDOWS, cells, LANES), BF),
        pltpu.VMEM((2, cells, channels), F32),
        pltpu.VMEM((rows, 160, channels), F32),
        pltpu.VMEM((rows, 160, channels), F32),
        pltpu.VMEM((rows, 96, channels), BF),
        pltpu.VMEM((rows, 96, channels), BF),
        pltpu.VMEM((ncol * chunk, 128), F32),
        pltpu.VMEM((ncol, chunk, 128), F32),
        pltpu.VMEM((chunk, 128), F32),
        pltpu.VMEM((nrow, chunk, 128), F32),
        pltpu.VMEM((ncol * chunk, 128), F32),
        pltpu.VMEM((WINDOWS, cells, LANES), F32),
        dma((2,)), dma((2,)), dma((8,)), dma((8,)), dma((8,)), dma((8,)), dma((2,)), dma((2,)),
        dma((ncol,)), dma((ncol,)), dma((nrow,)), dma((nrow,)), dma((ncol,)), dma((ncol,)),
    ]
    vmem = pl.BlockSpec(memory_space=pltpu.VMEM)
    return pl.pallas_call(
        functools.partial(kernel, nrow, ncol, chunk, owners, scale),
        out_shape=(
            jax.ShapeDtypeStruct((DISP, rows, cols, feats), BF),
            jax.ShapeDtypeStruct(weight.shape, F32),
            jax.ShapeDtypeStruct(left.shape, BF),
            jax.ShapeDtypeStruct(right.shape, BF),
        ),
        in_specs=[vmem] * 4,
        out_specs=(vmem,) * 4,
        scratch_shapes=scratch,
        compiler_params=pltpu.CompilerParams(
            collective_id=0, has_side_effects=True, vmem_limit_bytes=56 * 1024 * 1024
        ),
        name="cost_volume",
    )(left, right, weight, cotangent)


def solution(mesh):
    in_specs = (P("row", "col", None), P("row", "col", None), P(), P(None, "row", "col", None))
    out_specs = (P(None, "row", "col", None), P(), P("row", "col", None), P("row", "col", None))
    return jax.shard_map(
        functools.partial(on_device, mesh.shape["row"], mesh.shape["col"]),
        mesh=mesh, in_specs=in_specs, out_specs=out_specs, check_vma=False,
    )
```

```python
import functools
import math

import jax
import jax.numpy as jnp
from jax import lax
from jax.experimental import pallas as pl
from jax.experimental.pallas import tpu as pltpu
from jax.sharding import PartitionSpec as P

DISP = 24
STEP = 4
OUT_D = 6
IN_D = OUT_D + 2
WINDOWS = DISP // OUT_D
LANES = 256
BF = jnp.bfloat16
F32 = jnp.float32
MESH = pl.DeviceIdType.MESH
NEIGHBOURS = [(dr, dc) for dr in (-1, 0, 1) for dc in (-1, 0, 1) if (dr, dc) != (0, 0)]


def dot(a, b, contract=((1,), (0,))):
    return lax.dot_general(a, b, (contract, ((), ())), preferred_element_type=F32)


def iota(shape, dim):
    return lax.broadcasted_iota(jnp.int32, shape, dim)


def kernel(
    nrow, ncol, chunk, owners, scale,
    l_ref, r_ref, w_ref, c_ref,
    cost_ref, wg_ref, lg_ref, rg_ref,
    rband, rf0, rf4, lf, sel, band_n, band_t, cs, vs, vt, edge_c, edge_v, halo_c, halo_v,
    gv, spread, racc0, racc4, back_send, back_recv, dsum, slots1, part2, slots2, full, obuf,
    sem_rs, sem_rr, sem_cs, sem_cr, sem_vs, sem_vr, sem_bs, sem_br,
    sem1_s, sem1_r, sem2_s, sem2_r, sem3_s, sem3_r,
):
    rows, cols, channels = l_ref.shape
    groups, feats = w_ref.shape[4], w_ref.shape[3]
    group_size = channels // groups
    cells = rows * cols
    row, col = lax.axis_index("row"), lax.axis_index("col")

    def at(dr, dc):
        return (lax.rem(row + dr + nrow, nrow), lax.rem(col + dc + ncol, ncol))

    barrier = pltpu.get_barrier_semaphore()

    def hello_col(step, carry):
        pl.semaphore_signal(barrier, inc=1, device_id=at(0, step), device_id_type=MESH)
        return carry

    def hello_row(step, carry):
        pl.semaphore_signal(barrier, inc=1, device_id=at(step, 0), device_id_type=MESH)
        return carry

    lax.fori_loop(1, ncol, hello_col, 0)
    lax.fori_loop(1, nrow, hello_row, 0)
    for dr, dc in NEIGHBOURS:
        if dr != 0 and dc != 0:
            pl.semaphore_signal(barrier, inc=1, device_id=at(dr, dc), device_id_type=MESH)
    pl.semaphore_wait(barrier, ncol - 1 + nrow - 1 + 4)

    def copy(src, dst, send, recv, target):
        return pltpu.make_async_remote_copy(
            src_ref=src, dst_ref=dst, send_sem=send, recv_sem=recv,
            device_id=target, device_id_type=MESH,
        )

    right_copies = [
        copy(r_ref, rband.at[:, 32:96], sem_rs.at[0], sem_rr.at[0], at(0, 1)),
        copy(r_ref.at[:, cols - 32 : cols], rband.at[:, 0:32], sem_rs.at[1], sem_rr.at[1], at(0, 2)),
    ]
    for c in right_copies:
        c.start()

    def halo_copies(body, edge, halo, send, recv):
        out = []
        for n, (dr, dc) in enumerate(NEIGHBOURS):
            if dc == 0:
                src = body.at[1, :, rows if dr == 1 else 1]
                dst = body.at[1, :, 0 if dr == 1 else rows + 1]
            else:
                src = edge.at[1 if dc == 1 else 0]
                dst = halo.at[0 if dc == 1 else 1, 1 - dr]
            out.append(copy(src, dst, send.at[n], recv.at[n], at(dr, dc)))
        return out

    def edge_pieces(body):
        first, last = [], []
        for k in range(WINDOWS):
            for h in range(rows):
                first.append(body[1, k, 1 + h, 0:16].astype(F32)[0:1])
                last.append(body[1, k, 1 + h, cols - 16 : cols].astype(F32)[15:16])
        return first, last

    def fill_edges(edge, body):
        for side, lines in enumerate(edge_pieces(body)):
            acc = jnp.zeros((16, LANES), F32)
            for n, line in enumerate(lines):
                acc = jnp.where(iota((16, LANES), 0) == n, line, acc)
            edge[side] = acc.astype(BF)

    def clear_outside(body, halo):
        for cond, u, h in ((row == 0, 0, 0), (row == nrow - 1, 2, rows + 1)):
            @pl.when(cond)
            def _():
                for k in range(WINDOWS):
                    body[1, k, h] = jnp.zeros((cols, LANES), BF)
                for side in range(2):
                    halo[side, u] = jnp.zeros((16, LANES), BF)
        for cond, side in ((col == 0, 0), (col == ncol - 1, 1)):
            @pl.when(cond)
            def _():
                for u in range(3):
                    halo[side, u] = jnp.zeros((16, LANES), BF)

    def write_shifts(body, halo):
        lines = [[halo[side, u].astype(F32) for u in range(3)] for side in range(2)]
        where = iota((cols, LANES), 0)
        for k in range(WINDOWS):
            for h in range(rows + 2):
                u, n = (0, rows - 1) if h == 0 else ((2, 0) if h == rows + 1 else (1, h - 1))
                n = n + rows * k
                mid = body[1, k, h].astype(F32)
                before = jnp.where(where == 0, lines[0][u][n : n + 1], pltpu.roll(mid, 1, 0))
                after = jnp.where(where == cols - 1, lines[1][u][n : n + 1], pltpu.roll(mid, cols - 1, 0))
                body[0, k, h] = before.astype(BF)
                body[2, k, h] = after.astype(BF)

    for k in range(WINDOWS):
        for h in range(rows):
            parts = []
            for j in range(IN_D):
                d = OUT_D * k - 1 + j
                parts.append(c_ref[d, h] if 0 <= d < DISP else jnp.zeros((feats, cols), BF))
            cs[1, k, 1 + h] = jnp.concatenate(parts, axis=0).T
    fill_edges(edge_c, cs)
    cot_copies = halo_copies(cs, edge_c, halo_c, sem_cs, sem_cr)
    for c in cot_copies:
        c.start()

    lf[...] = l_ref[...].astype(F32)
    for i in range(OUT_D):
        r = iota((channels, LANES), 0) + i * channels
        sel[i] = jnp.where(r // group_size == iota((channels, LANES), 1), 1.0, 0.0).astype(BF)
    g_idx = iota((groups, IN_D * LANES), 0)
    lane = iota((groups, IN_D * LANES), 1)
    banded = jnp.zeros((9 * feats, IN_D * LANES), F32)
    for a in range(3):
        tap = jnp.where(
            (lane % LANES == (lane // LANES + a - 2) * groups + g_idx) & (lane % LANES < OUT_D * groups)
            & (lane // LANES + a >= 2), 1.0, 0.0
        ).astype(BF)
        wa = w_ref[a].astype(F32).reshape(9 * feats, groups).astype(BF)
        banded = banded + dot(wa, tap)
    for n in range(9):
        tall = [banded[feats * n : feats * (n + 1), LANES * j : LANES * (j + 1)] for j in range(IN_D)]
        tall = jnp.concatenate(tall, axis=0)
        band_t[LANES * n : LANES * (n + 1)] = tall.astype(BF)
        band_n[LANES * n : LANES * (n + 1)] = tall.T.astype(BF)

    for c in right_copies:
        c.wait_recv()
    @pl.when(col < 1)
    def _():
        rband[:, 32:96] = jnp.zeros((rows, 64, channels), BF)

    @pl.when(col < 2)
    def _():
        rband[:, 0:32] = jnp.zeros((rows, 32, channels), BF)

    for h in range(rows):
        rf0[h, 0:96] = rband[h].astype(F32)
        rf0[h, 96:160] = r_ref[h].astype(F32)
        rf4[h, 0:152] = rf0[h, 4:156]
        rf4[h, 152:160] = rf0[h, 152:160]

    def shifted(k, i, h=None):
        start = pl.multiple_of(96 - STEP * (OUT_D * k + i) - (STEP if i % 2 else 0), 8)
        src = rf4 if i % 2 else rf0
        if h is None:
            return src[:, pl.ds(start, cols)]
        return src[h, pl.ds(start, cols)]

    def volume(k, carry):
        acc = jnp.zeros((cells, LANES), F32)
        for i in range(OUT_D):
            product = (lf[...] * shifted(k, i)).astype(BF).reshape(cells, channels)
            acc = acc + dot(product, sel[i])
        acc = (acc * (1.0 / group_size)).astype(BF)
        vs[1, k, 1 : rows + 1] = acc.reshape(rows, cols, LANES)
        vt[k] = acc.T
        return carry

    lax.fori_loop(0, WINDOWS, volume, 0)
    fill_edges(edge_v, vs)
    vol_copies = halo_copies(vs, edge_v, halo_v, sem_vs, sem_vr)
    for c in vol_copies:
        c.start()

    for c in cot_copies:
        c.wait_recv()
    clear_outside(cs, halo_c)
    write_shifts(cs, halo_c)

    dsum[9 * groups :] = jnp.zeros((dsum.shape[0] - 9 * groups, 128), F32)

    def kernel_grad(n, carry):
        t, hb = 2 - n % 3, 2 - n // 3
        acc = jnp.zeros((LANES, LANES), F32)
        for k in range(WINDOWS):
            acc = acc + dot(vt[k], cs[t, k, pl.ds(hb, rows)].reshape(cells, LANES))
        total = acc[0:groups]
        for i in range(1, OUT_D):
            total = total + pltpu.roll(acc[groups * i : groups * (i + 1)], LANES - feats * i, 1)
        dsum[pl.ds(pl.multiple_of(n * groups, 8), groups)] = total[:, 0:128]
        return carry

    lax.fori_loop(0, 9, kernel_grad, 0)

    own_rows = pl.ds(pl.multiple_of(col * chunk, 8), chunk)

    def send1(step, carry):
        r, c = at(0, step)

        @pl.when(c < owners)
        def _():
            copy(
                dsum.at[pl.ds(pl.multiple_of(c * chunk, 8), chunk)], slots1.at[col],
                sem1_s.at[step], sem1_r.at[col], (r, c),
            ).start()
        return carry

    lax.fori_loop(1, ncol, send1, 0)

    def grad_volume(k, carry):
        taps = []
        for b in range(3):
            for e in range(3):
                taps.append(cs[2 - e, k, 2 - b : 2 - b + rows].reshape(cells, LANES))
        gv[k] = dot(jnp.concatenate(taps, axis=1), band_t[...]).astype(BF)
        return carry

    lax.fori_loop(0, WINDOWS, grad_volume, 0)

    @pl.when(col < owners)
    def _():
        slots1[col] = dsum[own_rows]

        def wait1(step, carry):
            _, c = at(0, step)
            copy(slots1.at[c], slots1.at[c], sem1_s.at[step], sem1_r.at[c], at(0, step)).wait_recv()
            return carry

        lax.fori_loop(1, ncol, wait1, 0)
        total = slots1[0]
        for q in range(1, ncol):
            total = total + slots1[q]
        part2[...] = total
        slots2[row] = total

        def send2(step, carry):
            copy(part2, slots2.at[row], sem2_s.at[step], sem2_r.at[row], at(step, 0)).start()
            return carry

        lax.fori_loop(1, nrow, send2, 0)

    racc0[...] = jnp.zeros_like(racc0)
    racc4[...] = jnp.zeros_like(racc4)
    lacc = spread.at[0]
    lacc[...] = jnp.zeros((cells, channels), F32)

    def feature_grads(k, carry):
        for i in range(OUT_D):
            spread[1] = dot(gv[k], sel[i], ((1,), (1,)))
            start = pl.multiple_of(96 - STEP * (OUT_D * k + i) - (STEP if i % 2 else 0), 8)
            acc = racc4 if i % 2 else racc0
            for h in range(rows):
                s = spread[1, cols * h : cols * (h + 1)]
                lacc[cols * h : cols * (h + 1)] += s * shifted(k, i, h)
                acc[h, pl.ds(start, cols)] += s * lf[h]
        return carry

    lax.fori_loop(0, WINDOWS, feature_grads, 0)
    inv = 1.0 / group_size
    lg_ref[...] = (lacc[...] * inv).reshape(rows, cols, channels).astype(BF)
    for h in range(rows):
        racc0[h, 4:156] += racc4[h, 0:152]
        back_send[h] = racc0[h, 0:96].astype(BF)
    back_copies = [
        copy(back_send.at[:, 32:96], back_recv.at[:, 0:64], sem_bs.at[0], sem_br.at[0], at(0, -1)),
        copy(back_send.at[:, 0:32], back_recv.at[:, 64:96], sem_bs.at[1], sem_br.at[1], at(0, -2)),
    ]
    for c in back_copies:
        c.start()

    @pl.when(col < owners)
    def _():
        def wait2(step, carry):
            r, _ = at(step, 0)
            copy(part2, slots2.at[r], sem2_s.at[step], sem2_r.at[r], at(step, 0)).wait_recv()
            return carry

        lax.fori_loop(1, nrow, wait2, 0)
        total = slots2[0]
        for q in range(1, nrow):
            total = total + slots2[q]
        full[own_rows] = total * scale

        def send3(step, carry):
            copy(full.at[own_rows], full.at[own_rows], sem3_s.at[step], sem3_r.at[col], at(0, step)).start()
            return carry

        lax.fori_loop(1, ncol, send3, 0)

    for c in vol_copies:
        c.wait_recv()
    clear_outside(vs, halo_v)
    write_shifts(vs, halo_v)

    def forward(k, carry):
        taps = []
        for b in range(3):
            for e in range(3):
                taps.append(vs[e, k, b : b + rows].reshape(cells, LANES))
        obuf[k] = dot(jnp.concatenate(taps, axis=1), band_n[...])
        return carry

    lax.fori_loop(0, WINDOWS, forward, 0)
    for h in range(rows):
        part = [obuf[k, cols * h : cols * (h + 1)].T for k in range(WINDOWS)]
        for k in range(WINDOWS):
            for i in range(OUT_D):
                j = i + 1
                value = part[k][feats * j : feats * (j + 1)]
                if i == 0 and k > 0:
                    value = value + part[k - 1][feats * (IN_D - 1) : feats * IN_D]
                if i == OUT_D - 1 and k < WINDOWS - 1:
                    value = value + part[k + 1][0:feats]
                cost_ref[OUT_D * k + i, h] = value.astype(BF)

    for c in back_copies:
        c.wait_recv()
    near = jnp.where(col < ncol - 1, 1.0, 0.0).astype(F32)
    far = jnp.where(col < ncol - 2, 1.0, 0.0).astype(F32)
    for h in range(rows):
        own = racc0[h, 96:160] + near * back_recv[h, 0:64].astype(F32)
        tail = own[32:64] + far * back_recv[h, 64:96].astype(F32)
        rg_ref[h, 0:32] = (own[0:32] * inv).astype(BF)
        rg_ref[h, 32:64] = (tail * inv).astype(BF)

    def wait3(step, carry):
        _, c = at(0, step)

        @pl.when(c < owners)
        def _():
            piece = full.at[pl.ds(pl.multiple_of(c * chunk, 8), chunk)]
            copy(piece, piece, sem3_s.at[step], sem3_r.at[c], at(0, step)).wait_recv()
        return carry

    lax.fori_loop(1, ncol, wait3, 0)
    for b in range(3):
        for e in range(3):
            block = full[groups * (3 * b + e) : groups * (3 * b + e + 1)].T
            for a in range(3):
                wg_ref[a, b, e] = block[feats * (2 - a) : feats * (3 - a)]

    for c in right_copies + cot_copies + vol_copies + back_copies:
        c.wait_send()

    def sent1(step, carry):
        _, c = at(0, step)

        @pl.when(c < owners)
        def _():
            copy(dsum.at[own_rows], slots1.at[col], sem1_s.at[step], sem1_r.at[col], at(0, step)).wait_send()
        return carry

    lax.fori_loop(1, ncol, sent1, 0)

    @pl.when(col < owners)
    def _():
        def sent2(step, carry):
            copy(part2, slots2.at[row], sem2_s.at[step], sem2_r.at[row], at(step, 0)).wait_send()
            return carry

        lax.fori_loop(1, nrow, sent2, 0)

        def sent3(step, carry):
            copy(full.at[own_rows], full.at[own_rows], sem3_s.at[step], sem3_r.at[col], at(0, step)).wait_send()
            return carry

        lax.fori_loop(1, ncol, sent3, 0)


def on_device(nrow, ncol, left, right, weight, cotangent):
    rows, cols, channels = left.shape
    groups, feats = weight.shape[3:]
    cells = rows * cols
    chunk = -(-9 * groups // ncol)
    chunk = -(-chunk // 16) * 16
    owners = -(-9 * groups // chunk)
    scale = 1.0 / math.sqrt(DISP * rows * nrow * cols * ncol)
    dma = pltpu.SemaphoreType.DMA
    body = pltpu.VMEM((3, WINDOWS, rows + 2, cols, LANES), BF)
    edge = pltpu.VMEM((2, 16, LANES), BF)
    halo = pltpu.VMEM((2, 3, 16, LANES), BF)
    scratch = [
        pltpu.VMEM((rows, 96, channels), BF),
        pltpu.VMEM((rows, 160, channels), F32),
        pltpu.VMEM((rows, 160, channels), F32),
        pltpu.VMEM((rows, cols, channels), F32),
        pltpu.VMEM((OUT_D, channels, LANES), BF),
        pltpu.VMEM((9 * LANES, LANES), BF),
        pltpu.VMEM((9 * LANES, LANES), BF),
        body, body,
        pltpu.VMEM((WINDOWS, LANES, cells), BF),
        edge, edge, halo, halo,
        pltpu.VMEM((WINDOWS, cells, LANES), BF),
        pltpu.VMEM((2, cells, channels), F32),
        pltpu.VMEM((rows, 160, channels), F32),
        pltpu.VMEM((rows, 160, channels), F32),
        pltpu.VMEM((rows, 96, channels), BF),
        pltpu.VMEM((rows, 96, channels), BF),
        pltpu.VMEM((ncol * chunk, 128), F32),
        pltpu.VMEM((ncol, chunk, 128), F32),
        pltpu.VMEM((chunk, 128), F32),
        pltpu.VMEM((nrow, chunk, 128), F32),
        pltpu.VMEM((ncol * chunk, 128), F32),
        pltpu.VMEM((WINDOWS, cells, LANES), F32),
        dma((2,)), dma((2,)), dma((8,)), dma((8,)), dma((8,)), dma((8,)), dma((2,)), dma((2,)),
        dma((ncol,)), dma((ncol,)), dma((nrow,)), dma((nrow,)), dma((ncol,)), dma((ncol,)),
    ]
    vmem = pl.BlockSpec(memory_space=pltpu.VMEM)
    cost, weight_grad, left_grad, right_grad = pl.pallas_call(
        functools.partial(kernel, nrow, ncol, chunk, owners, scale),
        out_shape=(
            jax.ShapeDtypeStruct((DISP, rows, feats, cols), BF),
            jax.ShapeDtypeStruct((3, 3, 3, feats, groups), F32),
            jax.ShapeDtypeStruct(left.shape, BF),
            jax.ShapeDtypeStruct(right.shape, BF),
        ),
        in_specs=[vmem] * 4,
        out_specs=(vmem,) * 4,
        scratch_shapes=scratch,
        compiler_params=pltpu.CompilerParams(
            collective_id=0, has_side_effects=True, vmem_limit_bytes=56 * 1024 * 1024
        ),
        name="cost_volume",
    )(left, right, jnp.swapaxes(weight, 3, 4), jnp.swapaxes(cotangent, 2, 3))
    return jnp.swapaxes(cost, 2, 3), jnp.swapaxes(weight_grad, 3, 4), left_grad, right_grad


def solution(mesh):
    in_specs = (P("row", "col", None), P("row", "col", None), P(), P(None, "row", "col", None))
    out_specs = (P(None, "row", "col", None), P(), P("row", "col", None), P("row", "col", None))
    return jax.shard_map(
        functools.partial(on_device, mesh.shape["row"], mesh.shape["col"]),
        mesh=mesh, in_specs=in_specs, out_specs=out_specs, check_vma=False,
    )
```

```python
import functools
import math

import jax
import jax.numpy as jnp
from jax import lax
from jax.experimental import pallas as pl
from jax.experimental.pallas import tpu as pltpu
from jax.sharding import PartitionSpec as P

DISP = 24
STEP = 4
OUT_D = 6
IN_D = OUT_D + 2
WINDOWS = DISP // OUT_D
LANES = 256
BF = jnp.bfloat16
F32 = jnp.float32
MESH = pl.DeviceIdType.MESH
NEIGHBOURS = [(dr, dc) for dr in (-1, 0, 1) for dc in (-1, 0, 1) if (dr, dc) != (0, 0)]


def dot(a, b, contract=((1,), (0,))):
    return lax.dot_general(a, b, (contract, ((), ())), preferred_element_type=F32)


def iota(shape, dim):
    return lax.broadcasted_iota(jnp.int32, shape, dim)


def kernel(
    nrow, ncol, scale,
    l_any, r_any, w_any, c_any,
    cost_any, wg_any, lg_any, rg_any,
    l_ref, r_ref, w_ref, c_ref, cost_ref, wg_ref, lg_ref, rg_ref,
    rband, rf0, rf4, lf, sel, band_n, band_t, cs, vs, vt, edge_c, edge_v, halo_c, halo_v,
    gv, spread, racc0, racc4, back_send, back_recv, dsum, slot_c, half, slots_r, part_m, slots_m,
    gathered, full, obuf,
    sem_in, sem_out, sem_rs, sem_rr, sem_cs, sem_cr, sem_vs, sem_vr, sem_bs, sem_br, sem_pair,
    sem1_s, sem1_r, sem2_s, sem2_r, sem3_s, sem3_r,
):
    rows, cols, channels = l_ref.shape
    groups, feats = w_ref.shape[4], w_ref.shape[3]
    group_size = channels // groups
    cells = rows * cols
    row, col = lax.axis_index("row"), lax.axis_index("col")
    pairs = ncol // 2
    pair, core = col // 2, lax.rem(col, 2)
    mate = (row, col + 1 - 2 * core)
    halfrows = dsum.shape[0] // 2
    chunk = halfrows // nrow

    def at(dr, dc):
        return (lax.rem(row + dr + nrow, nrow), lax.rem(col + dc + ncol, ncol))

    def along(step):
        return (row, lax.rem(pair + step, pairs) * 2 + core)

    barrier = pltpu.get_barrier_semaphore()
    partners = [at(dr, dc) for dr, dc in NEIGHBOURS if dc != 0]
    partners += [at(step, 0) for step in range(1, nrow)] + [along(step) for step in range(1, pairs)]
    for partner in partners:
        pl.semaphore_signal(barrier, inc=1, device_id=partner, device_id_type=MESH)
    loads = [
        pltpu.make_async_copy(src, dst, sem_in.at[n])
        for n, (src, dst) in enumerate(((c_any, c_ref), (w_any, w_ref), (l_any, l_ref), (r_any, r_ref)))
    ]
    for load in loads:
        load.start()
    pl.semaphore_wait(barrier, len(partners))

    def copy(src, dst, send, recv, target):
        return pltpu.make_async_remote_copy(
            src_ref=src, dst_ref=dst, send_sem=send, recv_sem=recv,
            device_id=target, device_id_type=MESH,
        )

    tail = r_any.at[:, cols - 32 : cols]
    near = copy(tail, rband.at[:, 64:96], sem_rs.at[0], sem_rr.at[0], at(0, 1))
    middle = copy(r_any.at[:, 0:32], rband.at[:, 32:64], sem_rs.at[1], sem_rr.at[1], at(0, 1))
    beyond = copy(tail, rband.at[:, 0:32], sem_rs.at[2], sem_rr.at[2], at(0, 2))
    forward_near = copy(rband.at[:, 64:96], rband.at[:, 0:32], sem_rs.at[3], sem_rr.at[2], mate)
    near.start()
    middle.start()

    @pl.when(core == 0)
    def _():
        beyond.start()

    def halo_copies(body, edge, halo, send, recv):
        out = []
        for n, (dr, dc) in enumerate(NEIGHBOURS):
            if dc == 0:
                src = body.at[1, :, rows if dr == 1 else 1]
                dst = body.at[1, :, 0 if dr == 1 else rows + 1]
            else:
                src = edge.at[1 if dc == 1 else 0]
                dst = halo.at[0 if dc == 1 else 1, 1 - dr]
            out.append(copy(src, dst, send.at[n], recv.at[n], at(dr, dc)))
        return out

    def edge_pieces(body):
        first, last = [], []
        for k in range(WINDOWS):
            for h in range(rows):
                first.append(body[1, k, 1 + h, 0:16].astype(F32)[0:1])
                last.append(body[1, k, 1 + h, cols - 16 : cols].astype(F32)[15:16])
        return first, last

    def fill_edges(edge, body):
        for side, lines in enumerate(edge_pieces(body)):
            acc = jnp.zeros((16, LANES), F32)
            for n, line in enumerate(lines):
                acc = jnp.where(iota((16, LANES), 0) == n, line, acc)
            edge[side] = acc.astype(BF)

    def clear_outside(body, halo):
        for cond, u, h in ((row == 0, 0, 0), (row == nrow - 1, 2, rows + 1)):
            @pl.when(cond)
            def _():
                for k in range(WINDOWS):
                    body[1, k, h] = jnp.zeros((cols, LANES), BF)
                for side in range(2):
                    halo[side, u] = jnp.zeros((16, LANES), BF)
        for cond, side in ((col == 0, 0), (col == ncol - 1, 1)):
            @pl.when(cond)
            def _():
                for u in range(3):
                    halo[side, u] = jnp.zeros((16, LANES), BF)

    def write_shifts(body, halo):
        lines = [[halo[side, u].astype(F32) for u in range(3)] for side in range(2)]
        where = iota((cols, LANES), 0)
        for k in range(WINDOWS):
            for h in range(rows + 2):
                u, n = (0, rows - 1) if h == 0 else ((2, 0) if h == rows + 1 else (1, h - 1))
                n = n + rows * k
                mid = body[1, k, h].astype(F32)
                before = jnp.where(where == 0, lines[0][u][n : n + 1], pltpu.roll(mid, 1, 0))
                after = jnp.where(where == cols - 1, lines[1][u][n : n + 1], pltpu.roll(mid, cols - 1, 0))
                body[0, k, h] = before.astype(BF)
                body[2, k, h] = after.astype(BF)

    loads[0].wait()
    for k in range(WINDOWS):
        for h in range(rows):
            parts = []
            for j in range(IN_D):
                d = OUT_D * k - 1 + j
                parts.append(c_ref[d, h] if 0 <= d < DISP else jnp.zeros((feats, cols), BF))
            cs[1, k, 1 + h] = jnp.concatenate(parts, axis=0).T
    fill_edges(edge_c, cs)
    cot_copies = halo_copies(cs, edge_c, halo_c, sem_cs, sem_cr)
    for c in cot_copies:
        c.start()

    loads[1].wait()
    loads[2].wait()
    loads[3].wait()
    lf[...] = l_ref[...].astype(F32)
    for i in range(OUT_D):
        r = iota((channels, LANES), 0) + i * channels
        sel[i] = jnp.where(r // group_size == iota((channels, LANES), 1), 1.0, 0.0).astype(BF)
    g_idx = iota((groups, IN_D * LANES), 0)
    lane = iota((groups, IN_D * LANES), 1)
    banded = jnp.zeros((9 * feats, IN_D * LANES), F32)
    for a in range(3):
        tap = jnp.where(
            (lane % LANES == (lane // LANES + a - 2) * groups + g_idx) & (lane % LANES < OUT_D * groups)
            & (lane // LANES + a >= 2), 1.0, 0.0
        ).astype(BF)
        wa = w_ref[a].astype(F32).reshape(9 * feats, groups).astype(BF)
        banded = banded + dot(wa, tap)
    for n in range(9):
        tall = [banded[feats * n : feats * (n + 1), LANES * j : LANES * (j + 1)] for j in range(IN_D)]
        tall = jnp.concatenate(tall, axis=0)
        band_t[LANES * n : LANES * (n + 1)] = tall.astype(BF)
        band_n[LANES * n : LANES * (n + 1)] = tall.T.astype(BF)

    for c in cot_copies:
        c.wait_recv()
    clear_outside(cs, halo_c)
    write_shifts(cs, halo_c)

    def grad_volume(k, carry):
        taps = []
        for b in range(3):
            for e in range(3):
                taps.append(cs[2 - e, k, 2 - b : 2 - b + rows].reshape(cells, LANES))
        gv[k] = dot(jnp.concatenate(taps, axis=1), band_t[...]).astype(BF)
        return carry

    lax.fori_loop(0, WINDOWS, grad_volume, 0)

    def widen(start, inside):
        for h in range(rows):
            block = rband[h, start : start + 32].astype(F32)
            rf0[h, start : start + 32] = jnp.where(inside, block, 0.0)
            stop = 152 if start == 64 else start + 32
            rf4[h, start:stop] = rf0[h, start + 4 : stop + 4]

    def shifted(k, i, h=None):
        start = pl.multiple_of(96 - STEP * (OUT_D * k + i) - (STEP if i % 2 else 0), 8)
        src = rf4 if i % 2 else rf0
        if h is None:
            return src[:, pl.ds(start, cols)]
        return src[h, pl.ds(start, cols)]

    def volume(k, carry):
        acc = jnp.zeros((cells, LANES), F32)
        for i in range(OUT_D):
            product = (lf[...] * shifted(k, i)).astype(BF).reshape(cells, channels)
            acc = acc + dot(product, sel[i])
        acc = (acc * (1.0 / group_size)).astype(BF)
        vs[1, k, 1 : rows + 1] = acc.reshape(rows, cols, LANES)
        vt[k] = acc.T
        return carry

    for h in range(rows):
        rf0[h, 96:160] = r_ref[h].astype(F32)
    near.wait_recv()

    @pl.when(core == 0)
    def _():
        forward_near.start()

    widen(64, col > 0)
    lax.fori_loop(0, 1, volume, 0)
    middle.wait_recv()
    widen(32, col > 0)
    lax.fori_loop(1, 2, volume, 0)
    beyond.wait_recv()
    widen(0, col > 1)
    lax.fori_loop(2, WINDOWS, volume, 0)
    fill_edges(edge_v, vs)
    vol_copies = halo_copies(vs, edge_v, halo_v, sem_vs, sem_vr)
    for c in vol_copies:
        c.start()

    dsum[9 * groups :] = jnp.zeros((dsum.shape[0] - 9 * groups, 128), F32)

    def kernel_grad(n, carry):
        t, hb = 2 - n % 3, 2 - n // 3
        acc = jnp.zeros((LANES, LANES), F32)
        for k in range(WINDOWS):
            acc = acc + dot(vt[k], cs[t, k, pl.ds(hb, rows)].reshape(cells, LANES))
        total = acc[0:groups]
        for i in range(1, OUT_D):
            total = total + pltpu.roll(acc[groups * i : groups * (i + 1)], LANES - feats * i, 1)
        dsum[pl.ds(pl.multiple_of(n * groups, 8), groups)] = total[:, 0:128]
        return carry

    lax.fori_loop(0, 9, kernel_grad, 0)

    my_half = pl.ds(pl.multiple_of(core * halfrows, 16), halfrows)
    pair_copy = copy(
        dsum.at[pl.ds(pl.multiple_of((1 - core) * halfrows, 16), halfrows)], slot_c,
        sem_pair.at[0], sem_pair.at[1], mate,
    )
    pair_copy.start()

    racc0[...] = jnp.zeros_like(racc0)
    racc4[...] = jnp.zeros_like(racc4)
    lacc = spread.at[0]
    lacc[...] = jnp.zeros((cells, channels), F32)

    def feature_grads(k, carry):
        for i in range(OUT_D):
            spread[1] = dot(gv[k], sel[i], ((1,), (1,)))
            start = pl.multiple_of(96 - STEP * (OUT_D * k + i) - (STEP if i % 2 else 0), 8)
            acc = racc4 if i % 2 else racc0
            for h in range(rows):
                s = spread[1, cols * h : cols * (h + 1)]
                lacc[cols * h : cols * (h + 1)] += s * shifted(k, i, h)
                acc[h, pl.ds(start, cols)] += s * lf[h]
        return carry

    lax.fori_loop(0, 2, feature_grads, 0)

    pair_copy.wait_recv()
    half[...] = dsum[my_half] + slot_c[...]
    row_copies = []
    for step in range(1, nrow):
        target = at(step, 0)
        row_copies.append(copy(
            half.at[pl.ds(pl.multiple_of(target[0] * chunk, 8), chunk)], slots_r.at[row],
            sem1_s.at[step], sem1_r.at[row], target,
        ))
        row_copies[-1].start()
    slots_r[row] = half[pl.ds(pl.multiple_of(row * chunk, 8), chunk)]
    lax.fori_loop(2, WINDOWS, feature_grads, 0)
    inv = 1.0 / group_size
    lg_ref[...] = (lacc[...] * inv).reshape(rows, cols, channels).astype(BF)
    left_out = pltpu.make_async_copy(lg_ref, lg_any, sem_out.at[2])
    left_out.start()
    for h in range(rows):
        racc0[h, 4:156] += racc4[h, 0:152]
        back_send[h] = racc0[h, 0:96].astype(BF)
    back_copies = [
        copy(back_send.at[:, 32:96], back_recv.at[:, 0:64], sem_bs.at[0], sem_br.at[0], at(0, -1)),
        copy(back_send.at[:, 0:32], back_recv.at[:, 64:96], sem_bs.at[1], sem_br.at[1], at(0, -2)),
    ]
    for c in back_copies:
        c.start()

    for step in range(1, nrow):
        r = at(step, 0)[0]
        copy(slots_r.at[r], slots_r.at[r], sem1_s.at[step], sem1_r.at[r], at(step, 0)).wait_recv()
    total = slots_r[0]
    for q in range(1, nrow):
        total = total + slots_r[q]
    if part_m.shape[0] > chunk:
        total = jnp.concatenate([total, jnp.zeros((part_m.shape[0] - chunk, 128), F32)], axis=0)
    part_m[...] = total.astype(BF)
    col_copies = []
    for step in range(1, pairs):
        col_copies.append(copy(part_m, slots_m.at[pair], sem2_s.at[step], sem2_r.at[pair], along(step)))
        col_copies[-1].start()
    slots_m[pair] = part_m[...]

    for c in vol_copies:
        c.wait_recv()
    clear_outside(vs, halo_v)
    write_shifts(vs, halo_v)

    def forward(k, carry):
        taps = []
        for b in range(3):
            for e in range(3):
                taps.append(vs[e, k, b : b + rows].reshape(cells, LANES))
        obuf[k] = dot(jnp.concatenate(taps, axis=1), band_n[...])
        return carry

    lax.fori_loop(0, WINDOWS, forward, 0)

    for step in range(1, pairs):
        p = lax.rem(pair + step, pairs)
        copy(part_m, slots_m.at[p], sem2_s.at[step], sem2_r.at[p], along(step)).wait_recv()
    total = slots_m[0].astype(F32)
    for q in range(1, pairs):
        total = total + slots_m[q].astype(F32)
    gathered[core, row] = (total * scale).astype(BF)
    gather_copies = []
    for step in range(1, nrow):
        mine = gathered.at[core, row]
        gather_copies.append(copy(mine, mine, sem3_s.at[step], sem3_r.at[row], at(step, 0)))
        gather_copies[-1].start()

    for h in range(rows):
        part = [obuf[k, cols * h : cols * (h + 1)].T for k in range(WINDOWS)]
        for k in range(WINDOWS):
            for i in range(OUT_D):
                j = i + 1
                value = part[k][feats * j : feats * (j + 1)]
                if i == 0 and k > 0:
                    value = value + part[k - 1][feats * (IN_D - 1) : feats * IN_D]
                if i == OUT_D - 1 and k < WINDOWS - 1:
                    value = value + part[k + 1][0:feats]
                cost_ref[OUT_D * k + i, h] = value.astype(BF)
    cost_out = pltpu.make_async_copy(cost_ref, cost_any, sem_out.at[0])
    cost_out.start()

    for c in back_copies:
        c.wait_recv()
    for h in range(rows):
        own = racc0[h, 96:160] + jnp.where(col < ncol - 1, back_recv[h, 0:64].astype(F32), 0.0)
        last = own[32:64] + jnp.where(col < ncol - 2, back_recv[h, 64:96].astype(F32), 0.0)
        rg_ref[h, 0:32] = (own[0:32] * inv).astype(BF)
        rg_ref[h, 32:64] = (last * inv).astype(BF)
    right_out = pltpu.make_async_copy(rg_ref, rg_any, sem_out.at[1])
    right_out.start()

    for step in range(1, nrow):
        r = at(step, 0)[0]
        theirs = gathered.at[core, r]
        copy(theirs, theirs, sem3_s.at[step], sem3_r.at[r], at(step, 0)).wait_recv()
    mate_copy = copy(gathered.at[core], gathered.at[core], sem_pair.at[2], sem_pair.at[3], mate)
    mate_copy.start()
    mate_copy.wait_recv()
    for side in range(2):
        for r in range(nrow):
            start = side * halfrows + r * chunk
            full[start : start + chunk] = gathered[side, r].astype(F32)[0:chunk]
    for b in range(3):
        for e in range(3):
            block = full[groups * (3 * b + e) : groups * (3 * b + e + 1)].T
            for a in range(3):
                wg_ref[a, b, e] = block[feats * (2 - a) : feats * (3 - a)]

    weight_out = pltpu.make_async_copy(wg_ref, wg_any, sem_out.at[3])
    weight_out.start()

    @pl.when(core == 0)
    def _():
        beyond.wait_send()
        forward_near.wait_send()

    sent = [near, middle, pair_copy, mate_copy] + cot_copies + vol_copies + back_copies
    for c in sent + row_copies + col_copies + gather_copies:
        c.wait_send()
    for c in (cost_out, right_out, left_out, weight_out):
        c.wait()


def on_device(nrow, ncol, left, right, weight, cotangent):
    rows, cols, channels = left.shape
    groups, feats = weight.shape[3:]
    cells = rows * cols
    halfrows = -(-9 * groups // (16 * nrow)) * 8 * nrow
    chunk = halfrows // nrow
    slab = -(-chunk // 16) * 16
    scale = 1.0 / math.sqrt(DISP * rows * nrow * cols * ncol)
    dma = pltpu.SemaphoreType.DMA
    body = pltpu.VMEM((3, WINDOWS, rows + 2, cols, LANES), BF)
    edge = pltpu.VMEM((2, 16, LANES), BF)
    halo = pltpu.VMEM((2, 3, 16, LANES), BF)
    outs = (
        jax.ShapeDtypeStruct((DISP, rows, feats, cols), BF),
        jax.ShapeDtypeStruct((3, 3, 3, feats, groups), F32),
        jax.ShapeDtypeStruct(left.shape, BF),
        jax.ShapeDtypeStruct(right.shape, BF),
    )
    args = (left, right, jnp.swapaxes(weight, 3, 4), jnp.swapaxes(cotangent, 2, 3))
    scratch = [pltpu.VMEM(a.shape, a.dtype) for a in args + outs] + [
        pltpu.VMEM((rows, 96, channels), BF),
        pltpu.VMEM((rows, 160, channels), F32),
        pltpu.VMEM((rows, 160, channels), F32),
        pltpu.VMEM((rows, cols, channels), F32),
        pltpu.VMEM((OUT_D, channels, LANES), BF),
        pltpu.VMEM((9 * LANES, LANES), BF),
        pltpu.VMEM((9 * LANES, LANES), BF),
        body, body,
        pltpu.VMEM((WINDOWS, LANES, cells), BF),
        edge, edge, halo, halo,
        pltpu.VMEM((WINDOWS, cells, LANES), BF),
        pltpu.VMEM((2, cells, channels), F32),
        pltpu.VMEM((rows, 160, channels), F32),
        pltpu.VMEM((rows, 160, channels), F32),
        pltpu.VMEM((rows, 96, channels), BF),
        pltpu.VMEM((rows, 96, channels), BF),
        pltpu.VMEM((2 * halfrows, 128), F32),
        pltpu.VMEM((halfrows, 128), F32),
        pltpu.VMEM((halfrows, 128), F32),
        pltpu.VMEM((nrow, chunk, 128), F32),
        pltpu.VMEM((slab, 128), BF),
        pltpu.VMEM((ncol // 2, slab, 128), BF),
        pltpu.VMEM((2, nrow, slab, 128), BF),
        pltpu.VMEM((2 * halfrows, 128), F32),
        pltpu.VMEM((WINDOWS, cells, LANES), F32),
        dma((4,)), dma((4,)), dma((4,)), dma((3,)), dma((8,)), dma((8,)), dma((8,)), dma((8,)),
        dma((2,)), dma((2,)), dma((4,)),
        dma((nrow,)), dma((nrow,)), dma((ncol // 2,)), dma((ncol // 2,)), dma((nrow,)), dma((nrow,)),
    ]
    anywhere = pl.BlockSpec(memory_space=pl.ANY)
    cost, weight_grad, left_grad, right_grad = pl.pallas_call(
        functools.partial(kernel, nrow, ncol, scale),
        out_shape=outs,
        in_specs=[anywhere] * 4,
        out_specs=(anywhere,) * 4,
        scratch_shapes=scratch,
        compiler_params=pltpu.CompilerParams(
            collective_id=0, has_side_effects=True, vmem_limit_bytes=56 * 1024 * 1024
        ),
        name="cost_volume",
    )(*args)
    return jnp.swapaxes(cost, 2, 3), jnp.swapaxes(weight_grad, 3, 4), left_grad, right_grad


def solution(mesh):
    in_specs = (P("row", "col", None), P("row", "col", None), P(), P(None, "row", "col", None))
    out_specs = (P(None, "row", "col", None), P(), P("row", "col", None), P("row", "col", None))
    return jax.shard_map(
        functools.partial(on_device, mesh.shape["row"], mesh.shape["col"]),
        mesh=mesh, in_specs=in_specs, out_specs=out_specs, check_vma=False,
    )
```

```python
import functools
import math

import jax
import jax.numpy as jnp
from jax import lax
from jax.experimental import pallas as pl
from jax.experimental.pallas import tpu as pltpu
from jax.sharding import PartitionSpec as P

DISP = 24
STEP = 4
OUT_D = 6
IN_D = OUT_D + 2
WINDOWS = DISP // OUT_D
LANES = 256
BF = jnp.bfloat16
F32 = jnp.float32
MESH = pl.DeviceIdType.MESH
NEIGHBOURS = [(dr, dc) for dr in (-1, 0, 1) for dc in (-1, 0, 1) if (dr, dc) != (0, 0)]


def dot(a, b, contract=((1,), (0,))):
    return lax.dot_general(a, b, (contract, ((), ())), preferred_element_type=F32)


def iota(shape, dim):
    return lax.broadcasted_iota(jnp.int32, shape, dim)


def kernel(
    nrow, ncol, scale,
    l_any, r_any, w_any, c_any,
    cost_ref, wg_ref, lg_ref, rg_ref,
    l_ref, r_ref, w_ref, c_ref,
    rband, rf0, rf4, lf, sel, band_n, band_t, cs, vs, vt, edge_c, edge_v, halo_c, halo_v,
    gv, spread, racc0, racc4, back_send, back_recv, dsum, slot_c, half, slots_r, part_m, slots_m,
    gathered, full, obuf,
    sem_in, sem_rs, sem_rr, sem_cs, sem_cr, sem_vs, sem_vr, sem_bs, sem_br, sem_pair,
    sem1_s, sem1_r, sem2_s, sem2_r, sem3_s, sem3_r,
):
    rows, cols, channels = l_ref.shape
    groups, feats = w_ref.shape[4], w_ref.shape[3]
    group_size = channels // groups
    cells = rows * cols
    row, col = lax.axis_index("row"), lax.axis_index("col")
    pairs = ncol // 2
    pair, core = col // 2, lax.rem(col, 2)
    mate = (row, col + 1 - 2 * core)
    halfrows = dsum.shape[0] // 2
    chunk = halfrows // nrow

    def at(dr, dc):
        return (lax.rem(row + dr + nrow, nrow), lax.rem(col + dc + ncol, ncol))

    def along(step):
        return (row, lax.rem(pair + step, pairs) * 2 + core)

    barrier = pltpu.get_barrier_semaphore()
    partners = [at(dr, dc) for dr, dc in NEIGHBOURS if dc != 0]
    partners += [at(step, 0) for step in range(1, nrow)] + [along(step) for step in range(1, pairs)]
    for partner in partners:
        pl.semaphore_signal(barrier, inc=1, device_id=partner, device_id_type=MESH)
    loads = [
        pltpu.make_async_copy(src, dst, sem_in.at[n])
        for n, (src, dst) in enumerate(((c_any, c_ref), (w_any, w_ref), (l_any, l_ref), (r_any, r_ref)))
    ]
    for load in loads:
        load.start()
    pl.semaphore_wait(barrier, len(partners))

    def copy(src, dst, send, recv, target):
        return pltpu.make_async_remote_copy(
            src_ref=src, dst_ref=dst, send_sem=send, recv_sem=recv,
            device_id=target, device_id_type=MESH,
        )

    tail = r_any.at[:, cols - 32 : cols]
    near = copy(tail, rband.at[:, 64:96], sem_rs.at[0], sem_rr.at[0], at(0, 1))
    middle = copy(r_any.at[:, 0:32], rband.at[:, 32:64], sem_rs.at[1], sem_rr.at[1], at(0, 1))
    beyond = copy(tail, rband.at[:, 0:32], sem_rs.at[2], sem_rr.at[2], at(0, 2))
    forward_near = copy(rband.at[:, 64:96], rband.at[:, 0:32], sem_rs.at[3], sem_rr.at[2], mate)
    near.start()
    middle.start()

    @pl.when(core == 0)
    def _():
        beyond.start()

    def halo_copies(body, edge, halo, send, recv):
        out = []
        for n, (dr, dc) in enumerate(NEIGHBOURS):
            if dc == 0:
                src = body.at[1, :, rows if dr == 1 else 1]
                dst = body.at[1, :, 0 if dr == 1 else rows + 1]
            else:
                src = edge.at[1 if dc == 1 else 0]
                dst = halo.at[0 if dc == 1 else 1, 1 - dr]
            out.append(copy(src, dst, send.at[n], recv.at[n], at(dr, dc)))
        return out

    def edge_pieces(body):
        first, last = [], []
        for k in range(WINDOWS):
            for h in range(rows):
                first.append(body[1, k, 1 + h, 0:16].astype(F32)[0:1])
                last.append(body[1, k, 1 + h, cols - 16 : cols].astype(F32)[15:16])
        return first, last

    def fill_edges(edge, body):
        for side, lines in enumerate(edge_pieces(body)):
            acc = jnp.zeros((16, LANES), F32)
            for n, line in enumerate(lines):
                acc = jnp.where(iota((16, LANES), 0) == n, line, acc)
            edge[side] = acc.astype(BF)

    def clear_outside(body, halo):
        for cond, u, h in ((row == 0, 0, 0), (row == nrow - 1, 2, rows + 1)):
            @pl.when(cond)
            def _():
                for k in range(WINDOWS):
                    body[1, k, h] = jnp.zeros((cols, LANES), BF)
                for side in range(2):
                    halo[side, u] = jnp.zeros((16, LANES), BF)
        for cond, side in ((col == 0, 0), (col == ncol - 1, 1)):
            @pl.when(cond)
            def _():
                for u in range(3):
                    halo[side, u] = jnp.zeros((16, LANES), BF)

    def write_shifts(body, halo):
        lines = [[halo[side, u].astype(F32) for u in range(3)] for side in range(2)]
        where = iota((cols, LANES), 0)
        for k in range(WINDOWS):
            for h in range(rows + 2):
                u, n = (0, rows - 1) if h == 0 else ((2, 0) if h == rows + 1 else (1, h - 1))
                n = n + rows * k
                mid = body[1, k, h].astype(F32)
                before = jnp.where(where == 0, lines[0][u][n : n + 1], pltpu.roll(mid, 1, 0))
                after = jnp.where(where == cols - 1, lines[1][u][n : n + 1], pltpu.roll(mid, cols - 1, 0))
                body[0, k, h] = before.astype(BF)
                body[2, k, h] = after.astype(BF)

    loads[0].wait()
    for k in range(WINDOWS):
        for h in range(rows):
            parts = []
            for j in range(IN_D):
                d = OUT_D * k - 1 + j
                parts.append(c_ref[d, h] if 0 <= d < DISP else jnp.zeros((feats, cols), BF))
            cs[1, k, 1 + h] = jnp.concatenate(parts, axis=0).T
    fill_edges(edge_c, cs)
    cot_copies = halo_copies(cs, edge_c, halo_c, sem_cs, sem_cr)
    for c in cot_copies:
        c.start()

    loads[1].wait()
    loads[2].wait()
    loads[3].wait()
    lf[...] = l_ref[...].astype(F32)
    for i in range(OUT_D):
        r = iota((channels, LANES), 0) + i * channels
        sel[i] = jnp.where(r // group_size == iota((channels, LANES), 1), 1.0, 0.0).astype(BF)
    g_idx = iota((groups, IN_D * LANES), 0)
    lane = iota((groups, IN_D * LANES), 1)
    banded = jnp.zeros((9 * feats, IN_D * LANES), F32)
    for a in range(3):
        tap = jnp.where(
            (lane % LANES == (lane // LANES + a - 2) * groups + g_idx) & (lane % LANES < OUT_D * groups)
            & (lane // LANES + a >= 2), 1.0, 0.0
        ).astype(BF)
        wa = w_ref[a].astype(F32).reshape(9 * feats, groups).astype(BF)
        banded = banded + dot(wa, tap)
    for n in range(9):
        tall = [banded[feats * n : feats * (n + 1), LANES * j : LANES * (j + 1)] for j in range(IN_D)]
        tall = jnp.concatenate(tall, axis=0)
        band_t[LANES * n : LANES * (n + 1)] = tall.astype(BF)
        band_n[LANES * n : LANES * (n + 1)] = tall.T.astype(BF)

    def widen(start, inside):
        for h in range(rows):
            block = rband[h, start : start + 32].astype(F32)
            rf0[h, start : start + 32] = jnp.where(inside, block, 0.0)
            stop = 152 if start == 64 else start + 32
            rf4[h, start:stop] = rf0[h, start + 4 : stop + 4]

    def shifted(k, i, h=None):
        start = pl.multiple_of(96 - STEP * (OUT_D * k + i) - (STEP if i % 2 else 0), 8)
        src = rf4 if i % 2 else rf0
        if h is None:
            return src[:, pl.ds(start, cols)]
        return src[h, pl.ds(start, cols)]

    def volume(k, carry):
        acc = jnp.zeros((cells, LANES), F32)
        for i in range(OUT_D):
            product = (lf[...] * shifted(k, i)).astype(BF).reshape(cells, channels)
            acc = acc + dot(product, sel[i])
        acc = (acc * (1.0 / group_size)).astype(BF)
        vs[1, k, 1 : rows + 1] = acc.reshape(rows, cols, LANES)
        vt[:, pl.ds(pl.multiple_of(k * cells, 128), cells)] = acc.T
        return carry

    for h in range(rows):
        rf0[h, 96:160] = r_ref[h].astype(F32)
    near.wait_recv()

    @pl.when(core == 0)
    def _():
        forward_near.start()

    widen(64, col > 0)
    lax.fori_loop(0, 1, volume, 0)
    middle.wait_recv()
    widen(32, col > 0)
    lax.fori_loop(1, 2, volume, 0)
    beyond.wait_recv()
    widen(0, col > 1)
    lax.fori_loop(2, WINDOWS, volume, 0)
    fill_edges(edge_v, vs)
    vol_copies = halo_copies(vs, edge_v, halo_v, sem_vs, sem_vr)
    for c in vol_copies:
        c.start()

    for c in cot_copies:
        c.wait_recv()
    clear_outside(cs, halo_c)
    write_shifts(cs, halo_c)

    dsum[9 * groups :] = jnp.zeros((dsum.shape[0] - 9 * groups, 128), F32)

    def kernel_grad(b, carry):
        for e in range(3):
            right = jnp.concatenate(
                [cs[2 - e, k, pl.ds(2 - b, rows)].reshape(cells, LANES) for k in range(WINDOWS)], axis=0
            )
            acc = dot(vt[...], right)
            total = acc[0:groups]
            for i in range(1, OUT_D):
                total = total + pltpu.roll(acc[groups * i : groups * (i + 1)], LANES - feats * i, 1)
            dsum[pl.ds(pl.multiple_of((3 * b + e) * groups, 8), groups)] = total[:, 0:128]
        return carry

    lax.fori_loop(0, 3, kernel_grad, 0)

    my_half = pl.ds(pl.multiple_of(core * halfrows, 16), halfrows)
    pair_copy = copy(
        dsum.at[pl.ds(pl.multiple_of((1 - core) * halfrows, 16), halfrows)], slot_c,
        sem_pair.at[0], sem_pair.at[1], mate,
    )
    pair_copy.start()

    def grad_volume(k, carry):
        taps = []
        for b in range(3):
            for e in range(3):
                taps.append(cs[2 - e, k, 2 - b : 2 - b + rows].reshape(cells, LANES))
        gv[k] = dot(jnp.concatenate(taps, axis=1), band_t[...]).astype(BF)
        return carry

    lax.fori_loop(0, WINDOWS, grad_volume, 0)

    pair_copy.wait_recv()
    half[...] = dsum[my_half] + slot_c[...]
    row_copies = []
    for step in range(1, nrow):
        target = at(step, 0)
        row_copies.append(copy(
            half.at[pl.ds(pl.multiple_of(target[0] * chunk, 8), chunk)], slots_r.at[row],
            sem1_s.at[step], sem1_r.at[row], target,
        ))
        row_copies[-1].start()
    slots_r[row] = half[pl.ds(pl.multiple_of(row * chunk, 8), chunk)]
    racc0[...] = jnp.zeros_like(racc0)
    racc4[...] = jnp.zeros_like(racc4)
    lacc = spread.at[0]
    lacc[...] = jnp.zeros((cells, channels), F32)

    def feature_grads(k, carry):
        for i in range(OUT_D):
            spread[1] = dot(gv[k], sel[i], ((1,), (1,)))
            start = pl.multiple_of(96 - STEP * (OUT_D * k + i) - (STEP if i % 2 else 0), 8)
            acc = racc4 if i % 2 else racc0
            for h in range(rows):
                s = spread[1, cols * h : cols * (h + 1)]
                lacc[cols * h : cols * (h + 1)] += s * shifted(k, i, h)
                acc[h, pl.ds(start, cols)] += s * lf[h]
        return carry

    lax.fori_loop(0, 2, feature_grads, 0)

    for step in range(1, nrow):
        r = at(step, 0)[0]
        copy(slots_r.at[r], slots_r.at[r], sem1_s.at[step], sem1_r.at[r], at(step, 0)).wait_recv()
    total = slots_r[0]
    for q in range(1, nrow):
        total = total + slots_r[q]
    if part_m.shape[0] > chunk:
        total = jnp.concatenate([total, jnp.zeros((part_m.shape[0] - chunk, 128), F32)], axis=0)
    part_m[...] = total.astype(BF)
    col_copies = []
    for step in range(1, pairs):
        col_copies.append(copy(part_m, slots_m.at[pair], sem2_s.at[step], sem2_r.at[pair], along(step)))
        col_copies[-1].start()
    slots_m[pair] = part_m[...]

    lax.fori_loop(2, WINDOWS, feature_grads, 0)
    inv = 1.0 / group_size
    lg_ref[...] = (lacc[...] * inv).reshape(rows, cols, channels).astype(BF)
    for h in range(rows):
        racc0[h, 4:156] += racc4[h, 0:152]
        back_send[h] = racc0[h, 0:96].astype(BF)
    back_copies = [
        copy(back_send.at[:, 32:96], back_recv.at[:, 0:64], sem_bs.at[0], sem_br.at[0], at(0, -1)),
        copy(back_send.at[:, 0:32], back_recv.at[:, 64:96], sem_bs.at[1], sem_br.at[1], at(0, -2)),
    ]
    for c in back_copies:
        c.start()

    for c in vol_copies:
        c.wait_recv()
    clear_outside(vs, halo_v)
    write_shifts(vs, halo_v)

    def forward(k, carry):
        taps = []
        for b in range(3):
            for e in range(3):
                taps.append(vs[e, k, b : b + rows].reshape(cells, LANES))
        obuf[k] = dot(jnp.concatenate(taps, axis=1), band_n[...])
        return carry

    lax.fori_loop(0, 2, forward, 0)

    for step in range(1, pairs):
        p = lax.rem(pair + step, pairs)
        copy(part_m, slots_m.at[p], sem2_s.at[step], sem2_r.at[p], along(step)).wait_recv()
    total = slots_m[0].astype(F32)
    for q in range(1, pairs):
        total = total + slots_m[q].astype(F32)
    gathered[core, row] = (total * scale).astype(BF)
    gather_copies = []
    for step in range(1, nrow):
        mine = gathered.at[core, row]
        gather_copies.append(copy(mine, mine, sem3_s.at[step], sem3_r.at[row], at(step, 0)))
        gather_copies[-1].start()

    lax.fori_loop(2, WINDOWS, forward, 0)

    for h in range(rows):
        part = [obuf[k, cols * h : cols * (h + 1)].T for k in range(WINDOWS)]
        for k in range(WINDOWS):
            for i in range(OUT_D):
                j = i + 1
                value = part[k][feats * j : feats * (j + 1)]
                if i == 0 and k > 0:
                    value = value + part[k - 1][feats * (IN_D - 1) : feats * IN_D]
                if i == OUT_D - 1 and k < WINDOWS - 1:
                    value = value + part[k + 1][0:feats]
                cost_ref[OUT_D * k + i, h] = value.astype(BF)

    for c in back_copies:
        c.wait_recv()
    for h in range(rows):
        own = racc0[h, 96:160] + jnp.where(col < ncol - 1, back_recv[h, 0:64].astype(F32), 0.0)
        last = own[32:64] + jnp.where(col < ncol - 2, back_recv[h, 64:96].astype(F32), 0.0)
        rg_ref[h, 0:32] = (own[0:32] * inv).astype(BF)
        rg_ref[h, 32:64] = (last * inv).astype(BF)

    for step in range(1, nrow):
        r = at(step, 0)[0]
        theirs = gathered.at[core, r]
        copy(theirs, theirs, sem3_s.at[step], sem3_r.at[r], at(step, 0)).wait_recv()
    mate_copy = copy(gathered.at[core], gathered.at[core], sem_pair.at[2], sem_pair.at[3], mate)
    mate_copy.start()
    mate_copy.wait_recv()
    for side in range(2):
        for r in range(nrow):
            start = side * halfrows + r * chunk
            full[start : start + chunk] = gathered[side, r].astype(F32)[0:chunk]
    for b in range(3):
        for e in range(3):
            block = full[groups * (3 * b + e) : groups * (3 * b + e + 1)].T
            for a in range(3):
                wg_ref[a, b, e] = block[feats * (2 - a) : feats * (3 - a)]


    @pl.when(core == 0)
    def _():
        beyond.wait_send()
        forward_near.wait_send()

    sent = [near, middle, pair_copy, mate_copy] + cot_copies + vol_copies + back_copies
    for c in sent + row_copies + col_copies + gather_copies:
        c.wait_send()


def on_device(nrow, ncol, left, right, weight, cotangent):
    rows, cols, channels = left.shape
    groups, feats = weight.shape[3:]
    cells = rows * cols
    halfrows = -(-9 * groups // (16 * nrow)) * 8 * nrow
    chunk = halfrows // nrow
    slab = -(-chunk // 16) * 16
    scale = 1.0 / math.sqrt(DISP * rows * nrow * cols * ncol)
    dma = pltpu.SemaphoreType.DMA
    body = pltpu.VMEM((3, WINDOWS, rows + 2, cols, LANES), BF)
    edge = pltpu.VMEM((2, 16, LANES), BF)
    halo = pltpu.VMEM((2, 3, 16, LANES), BF)
    outs = (
        jax.ShapeDtypeStruct((DISP, rows, feats, cols), BF),
        jax.ShapeDtypeStruct((3, 3, 3, feats, groups), F32),
        jax.ShapeDtypeStruct(left.shape, BF),
        jax.ShapeDtypeStruct(right.shape, BF),
    )
    args = (left, right, jnp.swapaxes(weight, 3, 4), jnp.swapaxes(cotangent, 2, 3))
    scratch = [pltpu.VMEM(a.shape, a.dtype) for a in args] + [
        pltpu.VMEM((rows, 96, channels), BF),
        pltpu.VMEM((rows, 160, channels), F32),
        pltpu.VMEM((rows, 160, channels), F32),
        pltpu.VMEM((rows, cols, channels), F32),
        pltpu.VMEM((OUT_D, channels, LANES), BF),
        pltpu.VMEM((9 * LANES, LANES), BF),
        pltpu.VMEM((9 * LANES, LANES), BF),
        body, body,
        pltpu.VMEM((LANES, WINDOWS * cells), BF),
        edge, edge, halo, halo,
        pltpu.VMEM((WINDOWS, cells, LANES), BF),
        pltpu.VMEM((2, cells, channels), F32),
        pltpu.VMEM((rows, 160, channels), F32),
        pltpu.VMEM((rows, 160, channels), F32),
        pltpu.VMEM((rows, 96, channels), BF),
        pltpu.VMEM((rows, 96, channels), BF),
        pltpu.VMEM((2 * halfrows, 128), F32),
        pltpu.VMEM((halfrows, 128), F32),
        pltpu.VMEM((halfrows, 128), F32),
        pltpu.VMEM((nrow, chunk, 128), F32),
        pltpu.VMEM((slab, 128), BF),
        pltpu.VMEM((ncol // 2, slab, 128), BF),
        pltpu.VMEM((2, nrow, slab, 128), BF),
        pltpu.VMEM((2 * halfrows, 128), F32),
        pltpu.VMEM((WINDOWS, cells, LANES), F32),
        dma((4,)), dma((4,)), dma((3,)), dma((8,)), dma((8,)), dma((8,)), dma((8,)),
        dma((2,)), dma((2,)), dma((4,)),
        dma((nrow,)), dma((nrow,)), dma((ncol // 2,)), dma((ncol // 2,)), dma((nrow,)), dma((nrow,)),
    ]
    anywhere = pl.BlockSpec(memory_space=pl.ANY)
    vmem = pl.BlockSpec(memory_space=pltpu.VMEM)
    results = pl.pallas_call(
        functools.partial(kernel, nrow, ncol, scale),
        out_shape=tuple(pltpu.VMEM(a.shape, a.dtype) for a in outs),
        in_specs=[anywhere] * 4,
        out_specs=(vmem,) * 4,
        scratch_shapes=scratch,
        compiler_params=pltpu.CompilerParams(
            collective_id=0, has_side_effects=True, vmem_limit_bytes=56 * 1024 * 1024
        ),
        name="cost_volume",
    )(*args)
    cost, weight_grad, left_grad, right_grad = results
    return jnp.swapaxes(cost, 2, 3), jnp.swapaxes(weight_grad, 3, 4), left_grad, right_grad


def solution(mesh):
    in_specs = (P("row", "col", None), P("row", "col", None), P(), P(None, "row", "col", None))
    out_specs = (P(None, "row", "col", None), P(), P("row", "col", None), P("row", "col", None))
    return jax.shard_map(
        functools.partial(on_device, mesh.shape["row"], mesh.shape["col"]),
        mesh=mesh, in_specs=in_specs, out_specs=out_specs, check_vma=False,
    )
```

```python
import functools
import math

import jax
import jax.numpy as jnp
from jax import lax
from jax.experimental import pallas as pl
from jax.experimental.pallas import tpu as pltpu
from jax.sharding import PartitionSpec as P

DISP = 24
STEP = 4
OUT_D = 6
IN_D = OUT_D + 2
WINDOWS = DISP // OUT_D
LANES = 256
BF = jnp.bfloat16
F32 = jnp.float32
MESH = pl.DeviceIdType.MESH
NEIGHBOURS = [(dr, dc) for dr in (-1, 0, 1) for dc in (-1, 0, 1) if (dr, dc) != (0, 0)]


def dot(a, b, contract=((1,), (0,))):
    return lax.dot_general(a, b, (contract, ((), ())), preferred_element_type=F32)


def iota(shape, dim):
    return lax.broadcasted_iota(jnp.int32, shape, dim)


def kernel(
    nrow, ncol, scale,
    l_any, r_any, w_any, c_any,
    cost_ref, wg_ref, lg_ref, rg_ref,
    l_ref, r_ref, w_ref, c_ref,
    rband, rf0, rf4, lf, sel, band_n, band_t, cs, vs, vt, edge_c, edge_v, halo_c, halo_v, line_send, line_recv,
    gv, spread, racc0, racc4, back_send, back_recv, dsum, slot_c, half, slots_r, part_m, slots_m,
    gathered, full, obuf,
    sem_in, sem_rs, sem_rr, sem_cs, sem_cr, sem_vs, sem_vr, sem_bs, sem_br, sem_pair,
    sem1_s, sem1_r, sem2_s, sem2_r, sem3_s, sem3_r,
):
    rows, cols, channels = l_ref.shape
    groups, feats = w_ref.shape[4], w_ref.shape[3]
    group_size = channels // groups
    cells = rows * cols
    row, col = lax.axis_index("row"), lax.axis_index("col")
    pairs = ncol // 2
    pair, core = col // 2, lax.rem(col, 2)
    mate = (row, col + 1 - 2 * core)
    halfrows = dsum.shape[0] // 2
    chunk = halfrows // nrow

    def at(dr, dc):
        return (lax.rem(row + dr + nrow, nrow), lax.rem(col + dc + ncol, ncol))

    def at_mate(step):
        return (lax.rem(row + step, nrow), mate[1])

    def along(step):
        return (row, lax.rem(pair + step, pairs) * 2 + core)

    barrier = pltpu.get_barrier_semaphore()
    partners = [at(dr, dc) for dr, dc in NEIGHBOURS if dc != 0]
    partners += [at(step, 0) for step in range(1, nrow)] + [along(step) for step in range(1, pairs)]
    loads = [
        pltpu.make_async_copy(src, dst, sem_in.at[n])
        for n, (src, dst) in enumerate(((c_any, c_ref), (w_any, w_ref), (l_any, l_ref), (r_any, r_ref)))
    ]
    for load in loads:
        load.start()
    partners += [at_mate(step) for step in range(1, nrow)]
    for partner in partners:
        pl.semaphore_signal(barrier, inc=1, device_id=partner, device_id_type=MESH)
    pl.semaphore_wait(barrier, len(partners))

    def copy(src, dst, send, recv, target):
        return pltpu.make_async_remote_copy(
            src_ref=src, dst_ref=dst, send_sem=send, recv_sem=recv,
            device_id=target, device_id_type=MESH,
        )

    tail = r_any.at[:, cols - 32 : cols]
    near = copy(tail, rband.at[:, 64:96], sem_rs.at[0], sem_rr.at[0], at(0, 1))
    middle = copy(r_any.at[:, 0:32], rband.at[:, 32:64], sem_rs.at[1], sem_rr.at[1], at(0, 1))
    beyond = copy(tail, rband.at[:, 0:32], sem_rs.at[2], sem_rr.at[2], at(0, 2))
    forward_near = copy(rband.at[:, 64:96], rband.at[:, 0:32], sem_rs.at[3], sem_rr.at[2], mate)
    near.start()
    middle.start()

    @pl.when(core == 0)
    def _():
        beyond.start()

    def halo_copies(body, edge, halo, send, recv, lines=None):
        out = []
        for n, (dr, dc) in enumerate(NEIGHBOURS):
            if dc == 0 and lines is not None:
                src = lines[0].at[1 if dr == 1 else 0]
                dst = lines[1].at[0 if dr == 1 else 1]
            elif dc == 0:
                src = body.at[1, :, rows if dr == 1 else 1]
                dst = body.at[1, :, 0 if dr == 1 else rows + 1]
            else:
                src = edge.at[1 if dc == 1 else 0]
                dst = halo.at[0 if dc == 1 else 1, 1 - dr]
            out.append(copy(src, dst, send.at[n], recv.at[n], at(dr, dc)))
        return out

    def edge_pieces(body):
        first, last = [], []
        for k in range(WINDOWS):
            for h in range(rows):
                first.append(body[1, k, 1 + h, 0:16].astype(F32)[0:1])
                last.append(body[1, k, 1 + h, cols - 16 : cols].astype(F32)[15:16])
        return first, last

    def fill_edges(edge, body):
        for side, lines in enumerate(edge_pieces(body)):
            acc = jnp.zeros((16, LANES), F32)
            for n, line in enumerate(lines):
                acc = jnp.where(iota((16, LANES), 0) == n, line, acc)
            edge[side] = acc.astype(BF)

    def clear_outside(body, halo):
        for cond, u, h in ((row == 0, 0, 0), (row == nrow - 1, 2, rows + 1)):
            @pl.when(cond)
            def _():
                for k in range(WINDOWS):
                    body[1, k, h] = jnp.zeros((cols, LANES), BF)
                for side in range(2):
                    halo[side, u] = jnp.zeros((16, LANES), BF)
        for cond, side in ((col == 0, 0), (col == ncol - 1, 1)):
            @pl.when(cond)
            def _():
                for u in range(3):
                    halo[side, u] = jnp.zeros((16, LANES), BF)

    def write_shifts(body, halo):
        lines = [[halo[side, u].astype(F32) for u in range(3)] for side in range(2)]
        where = iota((cols, LANES), 0)
        for k in range(WINDOWS):
            for h in range(rows + 2):
                u, n = (0, rows - 1) if h == 0 else ((2, 0) if h == rows + 1 else (1, h - 1))
                n = n + rows * k
                mid = body[1, k, h].astype(F32)
                before = jnp.where(where == 0, lines[0][u][n : n + 1], pltpu.roll(mid, 1, 0))
                after = jnp.where(where == cols - 1, lines[1][u][n : n + 1], pltpu.roll(mid, cols - 1, 0))
                body[0, k, h] = before.astype(BF)
                body[2, k, h] = after.astype(BF)

    loads[0].wait()
    for k in range(WINDOWS):
        for h in range(rows):
            parts = []
            for j in range(IN_D):
                d = OUT_D * k - 1 + j
                parts.append(c_ref[d, h] if 0 <= d < DISP else jnp.zeros((feats, cols), BF))
            cs[1, k, 1 + h] = jnp.concatenate(parts, axis=0).T
    fill_edges(edge_c, cs)
    for side, h in enumerate((0, rows - 1)):
        line_send[side] = jnp.concatenate([c_ref[d, h] for d in range(DISP)], axis=0).T
    cot_copies = halo_copies(cs, edge_c, halo_c, sem_cs, sem_cr, (line_send, line_recv))

    loads[1].wait()
    loads[2].wait()
    loads[3].wait()
    lf[...] = l_ref[...].astype(F32)
    for i in range(OUT_D):
        r = iota((channels, LANES), 0) + i * channels
        sel[i] = jnp.where(r // group_size == iota((channels, LANES), 1), 1.0, 0.0).astype(BF)
    g_idx = iota((groups, IN_D * LANES), 0)
    lane = iota((groups, IN_D * LANES), 1)
    banded = jnp.zeros((9 * feats, IN_D * LANES), F32)
    for a in range(3):
        tap = jnp.where(
            (lane % LANES == (lane // LANES + a - 2) * groups + g_idx) & (lane % LANES < OUT_D * groups)
            & (lane // LANES + a >= 2), 1.0, 0.0
        ).astype(BF)
        wa = w_ref[a].astype(F32).reshape(9 * feats, groups).astype(BF)
        banded = banded + dot(wa, tap)
    for n in range(9):
        tall = [banded[feats * n : feats * (n + 1), LANES * j : LANES * (j + 1)] for j in range(IN_D)]
        tall = jnp.concatenate(tall, axis=0)
        band_t[LANES * n : LANES * (n + 1)] = tall.astype(BF)
        band_n[LANES * n : LANES * (n + 1)] = tall.T.astype(BF)

    def widen(start, inside):
        for h in range(rows):
            block = rband[h, start : start + 32].astype(F32)
            rf0[h, start : start + 32] = jnp.where(inside, block, 0.0)
            stop = 152 if start == 64 else start + 32
            rf4[h, start:stop] = rf0[h, start + 4 : stop + 4]

    def shifted(k, i, h=None):
        start = pl.multiple_of(96 - STEP * (OUT_D * k + i) - (STEP if i % 2 else 0), 8)
        src = rf4 if i % 2 else rf0
        if h is None:
            return src[:, pl.ds(start, cols)]
        return src[h, pl.ds(start, cols)]

    def volume(k, carry):
        acc = jnp.zeros((cells, LANES), F32)
        for i in range(OUT_D):
            product = (lf[...] * shifted(k, i)).astype(BF).reshape(cells, channels)
            acc = acc + dot(product, sel[i])
        acc = (acc * (1.0 / group_size)).astype(BF)
        vs[1, k, 1 : rows + 1] = acc.reshape(rows, cols, LANES)
        vt[:, pl.ds(pl.multiple_of(k * cells, 128), cells)] = acc.T
        return carry

    for h in range(rows):
        rf0[h, 96:160] = r_ref[h].astype(F32)
    near.wait_recv()

    @pl.when(core == 0)
    def _():
        forward_near.start()

    for c in cot_copies:
        c.start()
    widen(64, col > 0)
    lax.fori_loop(0, 1, volume, 0)
    middle.wait_recv()
    widen(32, col > 0)
    lax.fori_loop(1, 2, volume, 0)
    beyond.wait_recv()
    widen(0, col > 1)
    lax.fori_loop(2, WINDOWS, volume, 0)
    fill_edges(edge_v, vs)
    vol_copies = halo_copies(vs, edge_v, halo_v, sem_vs, sem_vr)
    for c in vol_copies:
        c.start()

    for c in cot_copies:
        c.wait_recv()
    for side, h in enumerate((0, rows + 1)):
        line = line_recv[side]
        blank = jnp.zeros((cols, feats), BF)
        for k in range(WINDOWS):
            lo, hi = feats * (OUT_D * k - 1), feats * (OUT_D * k + OUT_D + 1)
            piece = line[:, max(lo, 0) : min(hi, feats * DISP)]
            if k == 0:
                piece = jnp.concatenate([blank, piece], axis=1)
            if k == WINDOWS - 1:
                piece = jnp.concatenate([piece, blank], axis=1)
            cs[1, k, h] = piece
    clear_outside(cs, halo_c)
    write_shifts(cs, halo_c)

    dsum[9 * groups :] = jnp.zeros((dsum.shape[0] - 9 * groups, 128), F32)

    def kernel_grad(b, carry):
        for e in range(3):
            right = jnp.concatenate(
                [cs[2 - e, k, pl.ds(2 - b, rows)].reshape(cells, LANES) for k in range(WINDOWS)], axis=0
            )
            acc = dot(vt[...], right)
            total = acc[0:groups]
            for i in range(1, OUT_D):
                total = total + pltpu.roll(acc[groups * i : groups * (i + 1)], LANES - feats * i, 1)
            dsum[pl.ds(pl.multiple_of((3 * b + e) * groups, 8), groups)] = total[:, 0:128]
        return carry

    lax.fori_loop(0, 3, kernel_grad, 0)

    my_half = pl.ds(pl.multiple_of(core * halfrows, 16), halfrows)
    pair_copy = copy(
        dsum.at[pl.ds(pl.multiple_of((1 - core) * halfrows, 16), halfrows)], slot_c,
        sem_pair.at[0], sem_pair.at[1], mate,
    )
    pair_copy.start()

    def grad_volume(k, carry):
        taps = []
        for b in range(3):
            for e in range(3):
                taps.append(cs[2 - e, k, 2 - b : 2 - b + rows].reshape(cells, LANES))
        gv[k] = dot(jnp.concatenate(taps, axis=1), band_t[...]).astype(BF)
        return carry

    lax.fori_loop(0, WINDOWS, grad_volume, 0)

    pair_copy.wait_recv()
    half[...] = dsum[my_half] + slot_c[...]
    row_copies = []
    for step in range(1, nrow):
        target = at(step, 0)
        row_copies.append(copy(
            half.at[pl.ds(pl.multiple_of(target[0] * chunk, 8), chunk)], slots_r.at[row],
            sem1_s.at[step], sem1_r.at[row], target,
        ))
        row_copies[-1].start()
    slots_r[row] = half[pl.ds(pl.multiple_of(row * chunk, 8), chunk)]
    racc0[...] = jnp.zeros_like(racc0)
    racc4[...] = jnp.zeros_like(racc4)
    lacc = spread.at[0]
    lacc[...] = jnp.zeros((cells, channels), F32)

    def feature_grads(k, carry):
        for i in range(OUT_D):
            spread[1] = dot(gv[k], sel[i], ((1,), (1,)))
            start = pl.multiple_of(96 - STEP * (OUT_D * k + i) - (STEP if i % 2 else 0), 8)
            acc = racc4 if i % 2 else racc0
            for h in range(rows):
                s = spread[1, cols * h : cols * (h + 1)]
                lacc[cols * h : cols * (h + 1)] += s * shifted(k, i, h)
                acc[h, pl.ds(start, cols)] += s * lf[h]
        return carry

    lax.fori_loop(0, 2, feature_grads, 0)

    for step in range(1, nrow):
        r = at(step, 0)[0]
        copy(slots_r.at[r], slots_r.at[r], sem1_s.at[step], sem1_r.at[r], at(step, 0)).wait_recv()
    total = slots_r[0]
    for q in range(1, nrow):
        total = total + slots_r[q]
    if part_m.shape[0] > chunk:
        total = jnp.concatenate([total, jnp.zeros((part_m.shape[0] - chunk, 128), F32)], axis=0)
    part_m[...] = total.astype(BF)
    col_copies = []
    for step in range(1, pairs):
        col_copies.append(copy(part_m, slots_m.at[pair], sem2_s.at[step], sem2_r.at[pair], along(step)))
        col_copies[-1].start()
    slots_m[pair] = part_m[...]

    lax.fori_loop(2, WINDOWS, feature_grads, 0)
    inv = 1.0 / group_size
    lg_ref[...] = (lacc[...] * inv).reshape(rows, cols, channels).astype(BF)
    for h in range(rows):
        racc0[h, 4:156] += racc4[h, 0:152]
        back_send[h] = racc0[h, 0:96].astype(BF)
    back_copies = [
        copy(back_send.at[:, 32:96], back_recv.at[:, 0:64], sem_bs.at[0], sem_br.at[0], at(0, -1)),
        copy(back_send.at[:, 0:32], back_recv.at[:, 64:96], sem_bs.at[1], sem_br.at[1], at(0, -2)),
    ]
    for c in back_copies:
        c.start()

    for c in vol_copies:
        c.wait_recv()
    clear_outside(vs, halo_v)
    write_shifts(vs, halo_v)

    def forward(k, carry):
        taps = []
        for b in range(3):
            for e in range(3):
                taps.append(vs[e, k, b : b + rows].reshape(cells, LANES))
        obuf[k] = dot(jnp.concatenate(taps, axis=1), band_n[...])
        return carry

    lax.fori_loop(0, 2, forward, 0)

    for step in range(1, pairs):
        p = lax.rem(pair + step, pairs)
        copy(part_m, slots_m.at[p], sem2_s.at[step], sem2_r.at[p], along(step)).wait_recv()
    total = slots_m[0].astype(F32)
    for q in range(1, pairs):
        total = total + slots_m[q].astype(F32)
    gathered[core, row] = (total * scale).astype(BF)
    gather_copies = []
    mine = gathered.at[core, row]
    for step in range(nrow):
        if step:
            gather_copies.append(copy(mine, mine, sem3_s.at[0, step], sem3_r.at[core, row], at(step, 0)))
        gather_copies.append(copy(mine, mine, sem3_s.at[1, step], sem3_r.at[core, row], at_mate(step)))
    for c in gather_copies:
        c.start()

    lax.fori_loop(2, WINDOWS, forward, 0)

    for h in range(rows):
        part = [obuf[k, cols * h : cols * (h + 1)].T for k in range(WINDOWS)]
        for k in range(WINDOWS):
            for i in range(OUT_D):
                j = i + 1
                value = part[k][feats * j : feats * (j + 1)]
                if i == 0 and k > 0:
                    value = value + part[k - 1][feats * (IN_D - 1) : feats * IN_D]
                if i == OUT_D - 1 and k < WINDOWS - 1:
                    value = value + part[k + 1][0:feats]
                cost_ref[OUT_D * k + i, h] = value.astype(BF)

    for c in back_copies:
        c.wait_recv()
    for h in range(rows):
        own = racc0[h, 96:160] + jnp.where(col < ncol - 1, back_recv[h, 0:64].astype(F32), 0.0)
        last = own[32:64] + jnp.where(col < ncol - 2, back_recv[h, 64:96].astype(F32), 0.0)
        rg_ref[h, 0:32] = (own[0:32] * inv).astype(BF)
        rg_ref[h, 32:64] = (last * inv).astype(BF)

    for step in range(nrow):
        r = lax.rem(row + step, nrow)
        if step:
            theirs = gathered.at[core, r]
            copy(theirs, theirs, sem3_s.at[0, step], sem3_r.at[core, r], at(step, 0)).wait_recv()
        theirs = gathered.at[1 - core, r]
        copy(theirs, theirs, sem3_s.at[1, step], sem3_r.at[1 - core, r], at_mate(step)).wait_recv()
    for side in range(2):
        for r in range(nrow):
            start = side * halfrows + r * chunk
            full[start : start + chunk] = gathered[side, r].astype(F32)[0:chunk]
    for b in range(3):
        for e in range(3):
            block = full[groups * (3 * b + e) : groups * (3 * b + e + 1)].T
            for a in range(3):
                wg_ref[a, b, e] = block[feats * (2 - a) : feats * (3 - a)]


    @pl.when(core == 0)
    def _():
        beyond.wait_send()
        forward_near.wait_send()

    sent = [near, middle, pair_copy] + cot_copies + vol_copies + back_copies
    for c in sent + row_copies + col_copies + gather_copies:
        c.wait_send()


def on_device(nrow, ncol, left, right, weight, cotangent):
    rows, cols, channels = left.shape
    groups, feats = weight.shape[3:]
    cells = rows * cols
    halfrows = -(-9 * groups // (16 * nrow)) * 8 * nrow
    chunk = halfrows // nrow
    slab = -(-chunk // 16) * 16
    scale = 1.0 / math.sqrt(DISP * rows * nrow * cols * ncol)
    dma = pltpu.SemaphoreType.DMA
    body = pltpu.VMEM((3, WINDOWS, rows + 2, cols, LANES), BF)
    edge = pltpu.VMEM((2, 16, LANES), BF)
    halo = pltpu.VMEM((2, 3, 16, LANES), BF)
    line = pltpu.VMEM((2, cols, DISP * feats), BF)
    outs = (
        jax.ShapeDtypeStruct((DISP, rows, feats, cols), BF),
        jax.ShapeDtypeStruct((3, 3, 3, feats, groups), F32),
        jax.ShapeDtypeStruct(left.shape, BF),
        jax.ShapeDtypeStruct(right.shape, BF),
    )
    args = (left, right, jnp.swapaxes(weight, 3, 4), jnp.swapaxes(cotangent, 2, 3))
    scratch = [pltpu.VMEM(a.shape, a.dtype) for a in args] + [
        pltpu.VMEM((rows, 96, channels), BF),
        pltpu.VMEM((rows, 160, channels), F32),
        pltpu.VMEM((rows, 160, channels), F32),
        pltpu.VMEM((rows, cols, channels), F32),
        pltpu.VMEM((OUT_D, channels, LANES), BF),
        pltpu.VMEM((9 * LANES, LANES), BF),
        pltpu.VMEM((9 * LANES, LANES), BF),
        body, body,
        pltpu.VMEM((LANES, WINDOWS * cells), BF),
        edge, edge, halo, halo, line, line,
        pltpu.VMEM((WINDOWS, cells, LANES), BF),
        pltpu.VMEM((2, cells, channels), F32),
        pltpu.VMEM((rows, 160, channels), F32),
        pltpu.VMEM((rows, 160, channels), F32),
        pltpu.VMEM((rows, 96, channels), BF),
        pltpu.VMEM((rows, 96, channels), BF),
        pltpu.VMEM((2 * halfrows, 128), F32),
        pltpu.VMEM((halfrows, 128), F32),
        pltpu.VMEM((halfrows, 128), F32),
        pltpu.VMEM((nrow, chunk, 128), F32),
        pltpu.VMEM((slab, 128), BF),
        pltpu.VMEM((ncol // 2, slab, 128), BF),
        pltpu.VMEM((2, nrow, slab, 128), BF),
        pltpu.VMEM((2 * halfrows, 128), F32),
        pltpu.VMEM((WINDOWS, cells, LANES), F32),
        dma((4,)), dma((4,)), dma((3,)), dma((8,)), dma((8,)), dma((8,)), dma((8,)),
        dma((2,)), dma((2,)), dma((2,)),
        dma((nrow,)), dma((nrow,)), dma((ncol // 2,)), dma((ncol // 2,)), dma((2, nrow)), dma((2, nrow)),
    ]
    anywhere = pl.BlockSpec(memory_space=pl.ANY)
    vmem = pl.BlockSpec(memory_space=pltpu.VMEM)
    results = pl.pallas_call(
        functools.partial(kernel, nrow, ncol, scale),
        out_shape=tuple(pltpu.VMEM(a.shape, a.dtype) for a in outs),
        in_specs=[anywhere] * 4,
        out_specs=(vmem,) * 4,
        scratch_shapes=scratch,
        compiler_params=pltpu.CompilerParams(
            collective_id=0, has_side_effects=True, vmem_limit_bytes=56 * 1024 * 1024
        ),
        name="cost_volume",
    )(*args)
    cost, weight_grad, left_grad, right_grad = results
    return jnp.swapaxes(cost, 2, 3), jnp.swapaxes(weight_grad, 3, 4), left_grad, right_grad


def solution(mesh):
    in_specs = (P("row", "col", None), P("row", "col", None), P(), P(None, "row", "col", None))
    out_specs = (P(None, "row", "col", None), P(), P("row", "col", None), P("row", "col", None))
    return jax.shard_map(
        functools.partial(on_device, mesh.shape["row"], mesh.shape["col"]),
        mesh=mesh, in_specs=in_specs, out_specs=out_specs, check_vma=False,
    )
```

```python
import functools
import math

import jax
import jax.numpy as jnp
from jax import lax
from jax.experimental import pallas as pl
from jax.experimental.pallas import tpu as pltpu
from jax.sharding import PartitionSpec as P

DISP = 24
STEP = 4
OUT_D = 6
IN_D = OUT_D + 2
WINDOWS = DISP // OUT_D
LANES = 256
BF = jnp.bfloat16
F32 = jnp.float32
MESH = pl.DeviceIdType.MESH
NEIGHBOURS = [(dr, dc) for dr in (-1, 0, 1) for dc in (-1, 0, 1) if (dr, dc) != (0, 0)]


def dot(a, b, contract=((1,), (0,))):
    return lax.dot_general(a, b, (contract, ((), ())), preferred_element_type=F32)


def iota(shape, dim):
    return lax.broadcasted_iota(jnp.int32, shape, dim)


def kernel(
    nrow, ncol, scale,
    l_any, r_any, w_any, c_any,
    cost_ref, wg_ref, lg_ref, rg_ref,
    l_ref, r_ref, w_ref, c_ref,
    rband, rf0, rf4, lf, sel, band_n, band_t, cs, vs, vt, edge_c, edge_v, halo_c, halo_v, line_send, line_recv,
    gv, spread, racc0, racc4, back_send, back_recv, dsum, slot_c, half, slots_r, part_m, slots_m,
    gathered, full, obuf,
    sem_in, sem_rs, sem_rr, sem_cs, sem_cr, sem_vs, sem_vr, sem_bs, sem_br, sem_pair,
    sem1_s, sem1_r, sem2_s, sem2_r, sem3_s, sem3_r,
):
    rows, cols, channels = l_ref.shape
    groups, feats = w_ref.shape[4], w_ref.shape[3]
    group_size = channels // groups
    cells = rows * cols
    row, col = lax.axis_index("row"), lax.axis_index("col")
    pairs = ncol // 2
    pair, core = col // 2, lax.rem(col, 2)
    mate = (row, col + 1 - 2 * core)
    halfrows = dsum.shape[0] // 2
    chunk = halfrows // nrow

    def at(dr, dc):
        return (lax.rem(row + dr + nrow, nrow), lax.rem(col + dc + ncol, ncol))

    def at_mate(step):
        return (lax.rem(row + step, nrow), mate[1])

    def along(step):
        return (row, lax.rem(pair + step, pairs) * 2 + core)

    barrier = pltpu.get_barrier_semaphore()
    partners = [at(dr, dc) for dr, dc in NEIGHBOURS if dc != 0]
    partners += [at(step, 0) for step in range(1, nrow)] + [along(step) for step in range(1, pairs)]
    loads = [
        pltpu.make_async_copy(src, dst, sem_in.at[n])
        for n, (src, dst) in enumerate(((c_any, c_ref), (w_any, w_ref), (l_any, l_ref), (r_any, r_ref)))
    ]
    for load in loads:
        load.start()
    partners += [at_mate(step) for step in range(1, nrow)]
    for partner in partners:
        pl.semaphore_signal(barrier, inc=1, device_id=partner, device_id_type=MESH)
    pl.semaphore_wait(barrier, len(partners))

    def copy(src, dst, send, recv, target):
        return pltpu.make_async_remote_copy(
            src_ref=src, dst_ref=dst, send_sem=send, recv_sem=recv,
            device_id=target, device_id_type=MESH,
        )

    tail = r_any.at[:, cols - 32 : cols]
    near = copy(tail, rband.at[:, 64:96], sem_rs.at[0], sem_rr.at[0], at(0, 1))
    middle = copy(r_any.at[:, 0:32], rband.at[:, 32:64], sem_rs.at[1], sem_rr.at[1], at(0, 1))
    beyond = copy(tail, rband.at[:, 0:32], sem_rs.at[2], sem_rr.at[2], at(0, 2))
    forward_near = copy(rband.at[:, 64:96], rband.at[:, 0:32], sem_rs.at[3], sem_rr.at[2], mate)
    @pl.when(core == 0)
    def _():
        beyond.start()

    near.start()
    middle.start()

    def halo_copies(body, edge, halo, send, recv, lines=None):
        out = []
        for n, (dr, dc) in enumerate(NEIGHBOURS):
            if dc == 0 and lines is not None:
                src = lines[0].at[1 if dr == 1 else 0]
                dst = lines[1].at[0 if dr == 1 else 1]
            elif dc == 0:
                src = body.at[1, :, rows if dr == 1 else 1]
                dst = body.at[1, :, 0 if dr == 1 else rows + 1]
            else:
                src = edge.at[1 if dc == 1 else 0]
                dst = halo.at[0 if dc == 1 else 1, 1 - dr]
            out.append(copy(src, dst, send.at[n], recv.at[n], at(dr, dc)))
        return out

    def edge_pieces(body):
        first, last = [], []
        for k in range(WINDOWS):
            for h in range(rows):
                first.append(body[1, k, 1 + h, 0:16].astype(F32)[0:1])
                last.append(body[1, k, 1 + h, cols - 16 : cols].astype(F32)[15:16])
        return first, last

    def fill_edges(edge, body):
        for side, lines in enumerate(edge_pieces(body)):
            acc = jnp.zeros((16, LANES), F32)
            for n, line in enumerate(lines):
                acc = jnp.where(iota((16, LANES), 0) == n, line, acc)
            edge[side] = acc.astype(BF)

    def clear_outside(body, halo):
        for cond, u, h in ((row == 0, 0, 0), (row == nrow - 1, 2, rows + 1)):
            @pl.when(cond)
            def _():
                for k in range(WINDOWS):
                    body[1, k, h] = jnp.zeros((cols, LANES), BF)
                for side in range(2):
                    halo[side, u] = jnp.zeros((16, LANES), BF)
        for cond, side in ((col == 0, 0), (col == ncol - 1, 1)):
            @pl.when(cond)
            def _():
                for u in range(3):
                    halo[side, u] = jnp.zeros((16, LANES), BF)

    def write_shifts(body, halo):
        lines = [[halo[side, u].astype(F32) for u in range(3)] for side in range(2)]
        where = iota((cols, LANES), 0)
        for k in range(WINDOWS):
            for h in range(rows + 2):
                u, n = (0, rows - 1) if h == 0 else ((2, 0) if h == rows + 1 else (1, h - 1))
                n = n + rows * k
                mid = body[1, k, h].astype(F32)
                before = jnp.where(where == 0, lines[0][u][n : n + 1], pltpu.roll(mid, 1, 0))
                after = jnp.where(where == cols - 1, lines[1][u][n : n + 1], pltpu.roll(mid, cols - 1, 0))
                body[0, k, h] = before.astype(BF)
                body[2, k, h] = after.astype(BF)

    loads[0].wait()
    for k in range(WINDOWS):
        for h in range(rows):
            parts = []
            for j in range(IN_D):
                d = OUT_D * k - 1 + j
                parts.append(c_ref[d, h] if 0 <= d < DISP else jnp.zeros((feats, cols), BF))
            cs[1, k, 1 + h] = jnp.concatenate(parts, axis=0).T
    fill_edges(edge_c, cs)
    for side, h in enumerate((0, rows - 1)):
        line_send[side] = jnp.concatenate([c_ref[d, h] for d in range(DISP)], axis=0).T
    cot_copies = halo_copies(cs, edge_c, halo_c, sem_cs, sem_cr, (line_send, line_recv))

    loads[1].wait()
    loads[2].wait()
    loads[3].wait()
    lf[...] = l_ref[...].astype(F32)
    for i in range(OUT_D):
        r = iota((channels, LANES), 0) + i * channels
        sel[i] = jnp.where(r // group_size == iota((channels, LANES), 1), 1.0, 0.0).astype(BF)
    g_idx = iota((groups, IN_D * LANES), 0)
    lane = iota((groups, IN_D * LANES), 1)
    banded = jnp.zeros((9 * feats, IN_D * LANES), F32)
    for a in range(3):
        tap = jnp.where(
            (lane % LANES == (lane // LANES + a - 2) * groups + g_idx) & (lane % LANES < OUT_D * groups)
            & (lane // LANES + a >= 2), 1.0, 0.0
        ).astype(BF)
        wa = w_ref[a].astype(F32).reshape(9 * feats, groups).astype(BF)
        banded = banded + dot(wa, tap)
    for n in range(9):
        tall = [banded[feats * n : feats * (n + 1), LANES * j : LANES * (j + 1)] for j in range(IN_D)]
        tall = jnp.concatenate(tall, axis=0)
        band_t[LANES * n : LANES * (n + 1)] = tall.astype(BF)
        band_n[LANES * n : LANES * (n + 1)] = tall.T.astype(BF)

    def widen(start, inside):
        for h in range(rows):
            block = rband[h, start : start + 32].astype(F32)
            rf0[h, start : start + 32] = jnp.where(inside, block, 0.0)
            stop = 152 if start == 64 else start + 32
            rf4[h, start:stop] = rf0[h, start + 4 : stop + 4]

    def shifted(k, i, h=None):
        start = pl.multiple_of(96 - STEP * (OUT_D * k + i) - (STEP if i % 2 else 0), 8)
        src = rf4 if i % 2 else rf0
        if h is None:
            return src[:, pl.ds(start, cols)]
        return src[h, pl.ds(start, cols)]

    def volume(k, carry):
        acc = jnp.zeros((cells, LANES), F32)
        for i in range(OUT_D):
            product = (lf[...] * shifted(k, i)).astype(BF).reshape(cells, channels)
            acc = acc + dot(product, sel[i])
        acc = (acc * (1.0 / group_size)).astype(BF)
        vs[1, k, 1 : rows + 1] = acc.reshape(rows, cols, LANES)
        vt[:, pl.ds(pl.multiple_of(k * cells, 128), cells)] = acc.T
        return carry

    for h in range(rows):
        rf0[h, 96:160] = r_ref[h].astype(F32)
    near.wait_recv()

    @pl.when(core == 0)
    def _():
        forward_near.start()

    for c in cot_copies:
        c.start()
    widen(64, col > 0)
    lax.fori_loop(0, 1, volume, 0)
    middle.wait_recv()
    widen(32, col > 0)
    lax.fori_loop(1, 2, volume, 0)
    beyond.wait_recv()
    widen(0, col > 1)
    lax.fori_loop(2, WINDOWS, volume, 0)
    fill_edges(edge_v, vs)
    vol_copies = halo_copies(vs, edge_v, halo_v, sem_vs, sem_vr)
    for c in vol_copies:
        c.start()

    for c in cot_copies:
        c.wait_recv()
    for side, h in enumerate((0, rows + 1)):
        line = line_recv[side]
        blank = jnp.zeros((cols, feats), BF)
        for k in range(WINDOWS):
            lo, hi = feats * (OUT_D * k - 1), feats * (OUT_D * k + OUT_D + 1)
            piece = line[:, max(lo, 0) : min(hi, feats * DISP)]
            if k == 0:
                piece = jnp.concatenate([blank, piece], axis=1)
            if k == WINDOWS - 1:
                piece = jnp.concatenate([piece, blank], axis=1)
            cs[1, k, h] = piece
    clear_outside(cs, halo_c)
    write_shifts(cs, halo_c)

    dsum[9 * groups :] = jnp.zeros((dsum.shape[0] - 9 * groups, 128), F32)

    def kernel_grad(b, carry):
        for e in range(3):
            right = jnp.concatenate(
                [cs[2 - e, k, pl.ds(2 - b, rows)].reshape(cells, LANES) for k in range(WINDOWS)], axis=0
            )
            acc = dot(vt[...], right)
            total = acc[0:groups]
            for i in range(1, OUT_D):
                total = total + pltpu.roll(acc[groups * i : groups * (i + 1)], LANES - feats * i, 1)
            dsum[pl.ds(pl.multiple_of((3 * b + e) * groups, 8), groups)] = total[:, 0:128]
        return carry

    lax.fori_loop(0, 3, kernel_grad, 0)

    my_half = pl.ds(pl.multiple_of(core * halfrows, 16), halfrows)
    pair_copy = copy(
        dsum.at[pl.ds(pl.multiple_of((1 - core) * halfrows, 16), halfrows)], slot_c,
        sem_pair.at[0], sem_pair.at[1], mate,
    )
    pair_copy.start()

    def grad_volume(k, carry):
        taps = []
        for b in range(3):
            for e in range(3):
                taps.append(cs[2 - e, k, 2 - b : 2 - b + rows].reshape(cells, LANES))
        gv[k] = dot(jnp.concatenate(taps, axis=1), band_t[...]).astype(BF)
        return carry

    lax.fori_loop(0, WINDOWS, grad_volume, 0)

    pair_copy.wait_recv()
    half[...] = dsum[my_half] + slot_c[...]
    row_copies = []
    for step in range(1, nrow):
        target = at(step, 0)
        row_copies.append(copy(
            half.at[pl.ds(pl.multiple_of(target[0] * chunk, 8), chunk)], slots_r.at[row],
            sem1_s.at[step], sem1_r.at[row], target,
        ))
        row_copies[-1].start()
    slots_r[row] = half[pl.ds(pl.multiple_of(row * chunk, 8), chunk)]
    racc0[...] = jnp.zeros_like(racc0)
    racc4[...] = jnp.zeros_like(racc4)
    lacc = spread.at[0]
    lacc[...] = jnp.zeros((cells, channels), F32)

    def feature_grads(k, carry):
        for i in range(OUT_D):
            spread[1] = dot(gv[k], sel[i], ((1,), (1,)))
            start = pl.multiple_of(96 - STEP * (OUT_D * k + i) - (STEP if i % 2 else 0), 8)
            acc = racc4 if i % 2 else racc0
            for h in range(rows):
                s = spread[1, cols * h : cols * (h + 1)]
                lacc[cols * h : cols * (h + 1)] += s * shifted(k, i, h)
                acc[h, pl.ds(start, cols)] += s * lf[h]
        return carry

    lax.fori_loop(0, 2, feature_grads, 0)

    for step in range(1, nrow):
        r = at(step, 0)[0]
        copy(slots_r.at[r], slots_r.at[r], sem1_s.at[step], sem1_r.at[r], at(step, 0)).wait_recv()
    total = slots_r[0]
    for q in range(1, nrow):
        total = total + slots_r[q]
    if part_m.shape[0] > chunk:
        total = jnp.concatenate([total, jnp.zeros((part_m.shape[0] - chunk, 128), F32)], axis=0)
    part_m[...] = total.astype(BF)
    col_copies = []
    for step in range(1, pairs):
        col_copies.append(copy(part_m, slots_m.at[pair], sem2_s.at[step], sem2_r.at[pair], along(step)))
        col_copies[-1].start()
    slots_m[pair] = part_m[...]

    lax.fori_loop(2, WINDOWS, feature_grads, 0)
    inv = 1.0 / group_size
    lg_ref[...] = (lacc[...] * inv).reshape(rows, cols, channels).astype(BF)
    for h in range(rows):
        racc0[h, 4:156] += racc4[h, 0:152]
        back_send[h] = racc0[h, 0:96].astype(BF)
    back_copies = [
        copy(back_send.at[:, 32:96], back_recv.at[:, 0:64], sem_bs.at[0], sem_br.at[0], at(0, -1)),
        copy(back_send.at[:, 0:32], back_recv.at[:, 64:96], sem_bs.at[1], sem_br.at[1], at(0, -2)),
    ]
    for c in back_copies:
        c.start()

    for c in vol_copies:
        c.wait_recv()
    clear_outside(vs, halo_v)
    write_shifts(vs, halo_v)

    def forward(k, carry):
        taps = []
        for b in range(3):
            for e in range(3):
                taps.append(vs[e, k, b : b + rows].reshape(cells, LANES))
        obuf[k] = dot(jnp.concatenate(taps, axis=1), band_n[...])
        return carry

    lax.fori_loop(0, 2, forward, 0)

    for step in range(1, pairs):
        p = lax.rem(pair + step, pairs)
        copy(part_m, slots_m.at[p], sem2_s.at[step], sem2_r.at[p], along(step)).wait_recv()
    total = slots_m[0].astype(F32)
    for q in range(1, pairs):
        total = total + slots_m[q].astype(F32)
    gathered[core, row] = (total * scale).astype(BF)
    gather_copies = []
    mine = gathered.at[core, row]
    for step in range(nrow):
        if step:
            gather_copies.append(copy(mine, mine, sem3_s.at[0, step], sem3_r.at[core, row], at(step, 0)))
        gather_copies.append(copy(mine, mine, sem3_s.at[1, step], sem3_r.at[core, row], at_mate(step)))
    for c in gather_copies:
        c.start()

    lax.fori_loop(2, WINDOWS, forward, 0)

    for h in range(rows):
        part = [obuf[k, cols * h : cols * (h + 1)].T for k in range(WINDOWS)]
        for k in range(WINDOWS):
            for i in range(OUT_D):
                j = i + 1
                value = part[k][feats * j : feats * (j + 1)]
                if i == 0 and k > 0:
                    value = value + part[k - 1][feats * (IN_D - 1) : feats * IN_D]
                if i == OUT_D - 1 and k < WINDOWS - 1:
                    value = value + part[k + 1][0:feats]
                cost_ref[OUT_D * k + i, h] = value.astype(BF)

    for c in back_copies:
        c.wait_recv()
    for h in range(rows):
        own = racc0[h, 96:160] + jnp.where(col < ncol - 1, back_recv[h, 0:64].astype(F32), 0.0)
        last = own[32:64] + jnp.where(col < ncol - 2, back_recv[h, 64:96].astype(F32), 0.0)
        rg_ref[h, 0:32] = (own[0:32] * inv).astype(BF)
        rg_ref[h, 32:64] = (last * inv).astype(BF)

    for step in range(nrow):
        r = lax.rem(row + step, nrow)
        if step:
            theirs = gathered.at[core, r]
            copy(theirs, theirs, sem3_s.at[0, step], sem3_r.at[core, r], at(step, 0)).wait_recv()
        theirs = gathered.at[1 - core, r]
        copy(theirs, theirs, sem3_s.at[1, step], sem3_r.at[1 - core, r], at_mate(step)).wait_recv()
    for side in range(2):
        for r in range(nrow):
            start = side * halfrows + r * chunk
            full[start : start + chunk] = gathered[side, r].astype(F32)[0:chunk]
    for b in range(3):
        for e in range(3):
            block = full[groups * (3 * b + e) : groups * (3 * b + e + 1)].T
            for a in range(3):
                wg_ref[a, b, e] = block[feats * (2 - a) : feats * (3 - a)]


    @pl.when(core == 0)
    def _():
        beyond.wait_send()
        forward_near.wait_send()

    sent = [near, middle, pair_copy] + cot_copies + vol_copies + back_copies
    for c in sent + row_copies + col_copies + gather_copies:
        c.wait_send()


def on_device(nrow, ncol, left, right, weight, cotangent):
    rows, cols, channels = left.shape
    groups, feats = weight.shape[3:]
    cells = rows * cols
    halfrows = -(-9 * groups // (16 * nrow)) * 8 * nrow
    chunk = halfrows // nrow
    slab = -(-chunk // 16) * 16
    scale = 1.0 / math.sqrt(DISP * rows * nrow * cols * ncol)
    dma = pltpu.SemaphoreType.DMA
    body = pltpu.VMEM((3, WINDOWS, rows + 2, cols, LANES), BF)
    edge = pltpu.VMEM((2, 16, LANES), BF)
    halo = pltpu.VMEM((2, 3, 16, LANES), BF)
    line = pltpu.VMEM((2, cols, DISP * feats), BF)
    outs = (
        jax.ShapeDtypeStruct((DISP, rows, feats, cols), BF),
        jax.ShapeDtypeStruct((3, 3, 3, feats, groups), F32),
        jax.ShapeDtypeStruct(left.shape, BF),
        jax.ShapeDtypeStruct(right.shape, BF),
    )
    args = (left, right, jnp.swapaxes(weight, 3, 4), jnp.swapaxes(cotangent, 2, 3))
    scratch = [pltpu.VMEM(a.shape, a.dtype) for a in args] + [
        pltpu.VMEM((rows, 96, channels), BF),
        pltpu.VMEM((rows, 160, channels), F32),
        pltpu.VMEM((rows, 160, channels), F32),
        pltpu.VMEM((rows, cols, channels), F32),
        pltpu.VMEM((OUT_D, channels, LANES), BF),
        pltpu.VMEM((9 * LANES, LANES), BF),
        pltpu.VMEM((9 * LANES, LANES), BF),
        body, body,
        pltpu.VMEM((LANES, WINDOWS * cells), BF),
        edge, edge, halo, halo, line, line,
        pltpu.VMEM((WINDOWS, cells, LANES), BF),
        pltpu.VMEM((2, cells, channels), F32),
        pltpu.VMEM((rows, 160, channels), F32),
        pltpu.VMEM((rows, 160, channels), F32),
        pltpu.VMEM((rows, 96, channels), BF),
        pltpu.VMEM((rows, 96, channels), BF),
        pltpu.VMEM((2 * halfrows, 128), F32),
        pltpu.VMEM((halfrows, 128), F32),
        pltpu.VMEM((halfrows, 128), F32),
        pltpu.VMEM((nrow, chunk, 128), F32),
        pltpu.VMEM((slab, 128), BF),
        pltpu.VMEM((ncol // 2, slab, 128), BF),
        pltpu.VMEM((2, nrow, slab, 128), BF),
        pltpu.VMEM((2 * halfrows, 128), F32),
        pltpu.VMEM((WINDOWS, cells, LANES), F32),
        dma((4,)), dma((4,)), dma((3,)), dma((8,)), dma((8,)), dma((8,)), dma((8,)),
        dma((2,)), dma((2,)), dma((2,)),
        dma((nrow,)), dma((nrow,)), dma((ncol // 2,)), dma((ncol // 2,)), dma((2, nrow)), dma((2, nrow)),
    ]
    anywhere = pl.BlockSpec(memory_space=pl.ANY)
    vmem = pl.BlockSpec(memory_space=pltpu.VMEM)
    results = pl.pallas_call(
        functools.partial(kernel, nrow, ncol, scale),
        out_shape=tuple(pltpu.VMEM(a.shape, a.dtype) for a in outs),
        in_specs=[anywhere] * 4,
        out_specs=(vmem,) * 4,
        scratch_shapes=scratch,
        compiler_params=pltpu.CompilerParams(
            collective_id=0, has_side_effects=True, vmem_limit_bytes=56 * 1024 * 1024
        ),
        name="cost_volume",
    )(*args)
    cost, weight_grad, left_grad, right_grad = results
    return jnp.swapaxes(cost, 2, 3), jnp.swapaxes(weight_grad, 3, 4), left_grad, right_grad


def solution(mesh):
    in_specs = (P("row", "col", None), P("row", "col", None), P(), P(None, "row", "col", None))
    out_specs = (P(None, "row", "col", None), P(), P("row", "col", None), P("row", "col", None))
    return jax.shard_map(
        functools.partial(on_device, mesh.shape["row"], mesh.shape["col"]),
        mesh=mesh, in_specs=in_specs, out_specs=out_specs, check_vma=False,
    )
```

```python
import functools
import math

import jax
import jax.numpy as jnp
from jax import lax
from jax.experimental import pallas as pl
from jax.experimental.pallas import tpu as pltpu
from jax.sharding import PartitionSpec as P

DISP = 24
STEP = 4
OUT_D = 6
IN_D = OUT_D + 2
WINDOWS = DISP // OUT_D
LANES = 256
BF = jnp.bfloat16
F32 = jnp.float32
MESH = pl.DeviceIdType.MESH
NEIGHBOURS = [(dr, dc) for dr in (-1, 0, 1) for dc in (-1, 0, 1) if (dr, dc) != (0, 0)]


def dot(a, b, contract=((1,), (0,))):
    return lax.dot_general(a, b, (contract, ((), ())), preferred_element_type=F32)


def iota(shape, dim):
    return lax.broadcasted_iota(jnp.int32, shape, dim)


def kernel(
    nrow, ncol, scale,
    l_any, r_any, w_any, c_any,
    cost_ref, wg_ref, lg_ref, rg_ref,
    l_ref, r_ref, w_ref, c_ref,
    rband, rf0, rf4, lf, sel, band_n, band_t, cs, vs, vt, edge_c, edge_v, halo_c, halo_v, line_send, line_recv,
    gv, spread, racc0, racc4, back_send, back_recv, dsum, slot_c, half, slots_r, part_m, slots_m,
    gathered, full, obuf,
    sem_in, sem_rs, sem_rr, sem_cs, sem_cr, sem_vs, sem_vr, sem_bs, sem_br, sem_pair,
    sem1_s, sem1_r, sem2_s, sem2_r, sem3_s, sem3_r,
):
    rows, cols, channels = l_ref.shape
    groups, feats = w_ref.shape[4], w_ref.shape[3]
    group_size = channels // groups
    cells = rows * cols
    row, col = lax.axis_index("row"), lax.axis_index("col")
    pairs = ncol // 2
    pair, core = col // 2, lax.rem(col, 2)
    mate = (row, col + 1 - 2 * core)
    halfrows = dsum.shape[0] // 2
    chunk = halfrows // nrow

    def at(dr, dc):
        return (lax.rem(row + dr + nrow, nrow), lax.rem(col + dc + ncol, ncol))

    def at_mate(step):
        return (lax.rem(row + step, nrow), mate[1])

    def along(step):
        return (row, lax.rem(pair + step, pairs) * 2 + core)

    barrier = pltpu.get_barrier_semaphore()
    partners = [at(dr, dc) for dr, dc in NEIGHBOURS if dc != 0]
    partners += [at(step, 0) for step in range(1, nrow)] + [along(step) for step in range(1, pairs)]
    loads = [
        pltpu.make_async_copy(src, dst, sem_in.at[n])
        for n, (src, dst) in enumerate(((c_any, c_ref), (w_any, w_ref), (l_any, l_ref), (r_any, r_ref)))
    ]
    for load in loads:
        load.start()
    partners += [at_mate(step) for step in range(1, nrow)]
    for partner in partners:
        pl.semaphore_signal(barrier, inc=1, device_id=partner, device_id_type=MESH)
    pl.semaphore_wait(barrier, len(partners))

    def copy(src, dst, send, recv, target):
        return pltpu.make_async_remote_copy(
            src_ref=src, dst_ref=dst, send_sem=send, recv_sem=recv,
            device_id=target, device_id_type=MESH,
        )

    tail = r_any.at[:, cols - 32 : cols]
    near = copy(tail, rband.at[:, 64:96], sem_rs.at[0], sem_rr.at[0], at(0, 1))
    middle = copy(r_any.at[:, 0:32], rband.at[:, 32:64], sem_rs.at[1], sem_rr.at[1], at(0, 1))
    beyond = copy(tail, rband.at[:, 0:32], sem_rs.at[2], sem_rr.at[2], at(0, 2))
    forward_near = copy(rband.at[:, 64:96], rband.at[:, 0:32], sem_rs.at[3], sem_rr.at[2], mate)
    @pl.when(core == 0)
    def _():
        beyond.start()

    near.start()
    middle.start()

    def halo_copies(body, edge, halo, send, recv, lines=None):
        out = []
        for n, (dr, dc) in enumerate(NEIGHBOURS):
            if dc == 0 and lines is not None:
                src = lines[0].at[1 if dr == 1 else 0]
                dst = lines[1].at[0 if dr == 1 else 1]
            elif dc == 0:
                src = body.at[1, :, rows if dr == 1 else 1]
                dst = body.at[1, :, 0 if dr == 1 else rows + 1]
            else:
                src = edge.at[1 if dc == 1 else 0]
                dst = halo.at[0 if dc == 1 else 1, 1 - dr]
            out.append(copy(src, dst, send.at[n], recv.at[n], at(dr, dc)))
        return out

    def edge_pieces(body):
        first, last = [], []
        for k in range(WINDOWS):
            for h in range(rows):
                first.append(body[1, k, 1 + h, 0:16].astype(F32)[0:1])
                last.append(body[1, k, 1 + h, cols - 16 : cols].astype(F32)[15:16])
        return first, last

    def fill_edges(edge, body):
        for side, lines in enumerate(edge_pieces(body)):
            acc = jnp.zeros((16, LANES), F32)
            for n, line in enumerate(lines):
                acc = jnp.where(iota((16, LANES), 0) == n, line, acc)
            edge[side] = acc.astype(BF)

    def clear_outside(body, halo):
        for cond, u, h in ((row == 0, 0, 0), (row == nrow - 1, 2, rows + 1)):
            @pl.when(cond)
            def _():
                for k in range(WINDOWS):
                    body[1, k, h] = jnp.zeros((cols, LANES), BF)
                for side in range(2):
                    halo[side, u] = jnp.zeros((16, LANES), BF)
        for cond, side in ((col == 0, 0), (col == ncol - 1, 1)):
            @pl.when(cond)
            def _():
                for u in range(3):
                    halo[side, u] = jnp.zeros((16, LANES), BF)

    def write_shifts(body, halo):
        lines = [[halo[side, u].astype(F32) for u in range(3)] for side in range(2)]
        where = iota((cols, LANES), 0)
        for k in range(WINDOWS):
            for h in range(rows + 2):
                u, n = (0, rows - 1) if h == 0 else ((2, 0) if h == rows + 1 else (1, h - 1))
                n = n + rows * k
                mid = body[1, k, h].astype(F32)
                before = jnp.where(where == 0, lines[0][u][n : n + 1], pltpu.roll(mid, 1, 0))
                after = jnp.where(where == cols - 1, lines[1][u][n : n + 1], pltpu.roll(mid, cols - 1, 0))
                body[0, k, h] = before.astype(BF)
                body[2, k, h] = after.astype(BF)

    loads[0].wait()
    for k in range(WINDOWS):
        for h in range(rows):
            parts = []
            for j in range(IN_D):
                d = OUT_D * k - 1 + j
                parts.append(c_ref[d, h] if 0 <= d < DISP else jnp.zeros((feats, cols), BF))
            cs[1, k, 1 + h] = jnp.concatenate(parts, axis=0).T
    fill_edges(edge_c, cs)
    for side, h in enumerate((0, rows - 1)):
        line_send[side] = jnp.concatenate([c_ref[d, h] for d in range(DISP)], axis=0).T
    cot_copies = halo_copies(cs, edge_c, halo_c, sem_cs, sem_cr, (line_send, line_recv))

    loads[1].wait()
    loads[2].wait()
    loads[3].wait()
    lf[...] = l_ref[...].astype(F32)
    for i in range(OUT_D):
        r = iota((channels, LANES), 0) + i * channels
        sel[i] = jnp.where(r // group_size == iota((channels, LANES), 1), 1.0, 0.0).astype(BF)
    g_idx = iota((groups, IN_D * LANES), 0)
    lane = iota((groups, IN_D * LANES), 1)
    banded = jnp.zeros((9 * feats, IN_D * LANES), F32)
    for a in range(3):
        tap = jnp.where(
            (lane % LANES == (lane // LANES + a - 2) * groups + g_idx) & (lane % LANES < OUT_D * groups)
            & (lane // LANES + a >= 2), 1.0, 0.0
        ).astype(BF)
        wa = w_ref[a].astype(F32).reshape(9 * feats, groups).astype(BF)
        banded = banded + dot(wa, tap)
    for n in range(9):
        tall = [banded[feats * n : feats * (n + 1), LANES * j : LANES * (j + 1)] for j in range(IN_D)]
        tall = jnp.concatenate(tall, axis=0)
        band_t[LANES * n : LANES * (n + 1)] = tall.astype(BF)
        band_n[LANES * n : LANES * (n + 1)] = tall.T.astype(BF)

    def widen(start, inside):
        for h in range(rows):
            block = rband[h, start : start + 32].astype(F32)
            rf0[h, start : start + 32] = jnp.where(inside, block, 0.0)
            stop = 152 if start == 64 else start + 32
            rf4[h, start:stop] = rf0[h, start + 4 : stop + 4]

    def shifted(k, i, h=None):
        start = pl.multiple_of(96 - STEP * (OUT_D * k + i) - (STEP if i % 2 else 0), 8)
        src = rf4 if i % 2 else rf0
        if h is None:
            return src[:, pl.ds(start, cols)]
        return src[h, pl.ds(start, cols)]

    def volume(k, carry):
        acc = jnp.zeros((cells, LANES), F32)
        for i in range(OUT_D):
            product = (lf[...] * shifted(k, i)).astype(BF).reshape(cells, channels)
            acc = acc + dot(product, sel[i])
        acc = (acc * (1.0 / group_size)).astype(BF)
        vs[1, k, 1 : rows + 1] = acc.reshape(rows, cols, LANES)
        vt[:, pl.ds(pl.multiple_of(k * cells, 128), cells)] = acc.T
        return carry

    for h in range(rows):
        rf0[h, 96:160] = r_ref[h].astype(F32)
    near.wait_recv()

    @pl.when(core == 0)
    def _():
        forward_near.start()

    for c in cot_copies:
        c.start()
    widen(64, col > 0)
    lax.fori_loop(0, 1, volume, 0)
    middle.wait_recv()
    widen(32, col > 0)
    lax.fori_loop(1, 2, volume, 0)
    beyond.wait_recv()
    widen(0, col > 1)
    lax.fori_loop(2, WINDOWS, volume, 0)
    fill_edges(edge_v, vs)
    vol_copies = halo_copies(vs, edge_v, halo_v, sem_vs, sem_vr)
    for c in vol_copies:
        c.start()

    for c in cot_copies:
        c.wait_recv()
    for side, h in enumerate((0, rows + 1)):
        line = line_recv[side]
        blank = jnp.zeros((cols, feats), BF)
        for k in range(WINDOWS):
            lo, hi = feats * (OUT_D * k - 1), feats * (OUT_D * k + OUT_D + 1)
            piece = line[:, max(lo, 0) : min(hi, feats * DISP)]
            if k == 0:
                piece = jnp.concatenate([blank, piece], axis=1)
            if k == WINDOWS - 1:
                piece = jnp.concatenate([piece, blank], axis=1)
            cs[1, k, h] = piece
    clear_outside(cs, halo_c)
    write_shifts(cs, halo_c)

    dsum[9 * groups :] = jnp.zeros((dsum.shape[0] - 9 * groups, 128), F32)

    def kernel_grad(b, carry):
        for e in range(3):
            right = jnp.concatenate(
                [cs[2 - e, k, pl.ds(2 - b, rows)].reshape(cells, LANES) for k in range(WINDOWS)], axis=0
            )
            acc = dot(vt[...], right)
            total = acc[0:groups]
            for i in range(1, OUT_D):
                total = total + pltpu.roll(acc[groups * i : groups * (i + 1)], LANES - feats * i, 1)
            dsum[pl.ds(pl.multiple_of((3 * b + e) * groups, 8), groups)] = total[:, 0:128]
        return carry

    lax.fori_loop(0, 3, kernel_grad, 0)

    my_half = pl.ds(pl.multiple_of(core * halfrows, 16), halfrows)
    pair_copy = copy(
        dsum.at[pl.ds(pl.multiple_of((1 - core) * halfrows, 16), halfrows)], slot_c,
        sem_pair.at[0], sem_pair.at[1], mate,
    )
    pair_copy.start()

    def grad_volume(k, carry):
        taps = []
        for b in range(3):
            for e in range(3):
                taps.append(cs[2 - e, k, 2 - b : 2 - b + rows].reshape(cells, LANES))
        gv[k] = dot(jnp.concatenate(taps, axis=1), band_t[...]).astype(BF)
        return carry

    lax.fori_loop(0, WINDOWS, grad_volume, 0)

    pair_copy.wait_recv()
    half[...] = dsum[my_half] + slot_c[...]
    row_copies = []
    for step in range(1, nrow):
        target = at(step, 0)
        row_copies.append(copy(
            half.at[pl.ds(pl.multiple_of(target[0] * chunk, 8), chunk)], slots_r.at[row],
            sem1_s.at[step], sem1_r.at[row], target,
        ))
        row_copies[-1].start()
    slots_r[row] = half[pl.ds(pl.multiple_of(row * chunk, 8), chunk)]
    racc0[...] = jnp.zeros_like(racc0)
    racc4[...] = jnp.zeros_like(racc4)
    lacc = spread.at[0]
    lacc[...] = jnp.zeros((cells, channels), F32)

    def feature_grads(k, carry):
        for i in range(OUT_D):
            spread[1] = dot(gv[k], sel[i], ((1,), (1,)))
            start = pl.multiple_of(96 - STEP * (OUT_D * k + i) - (STEP if i % 2 else 0), 8)
            acc = racc4 if i % 2 else racc0
            for h in range(rows):
                s = spread[1, cols * h : cols * (h + 1)]
                lacc[cols * h : cols * (h + 1)] += s * shifted(k, i, h)
                acc[h, pl.ds(start, cols)] += s * lf[h]
        return carry

    lax.fori_loop(0, 2, feature_grads, 0)

    for step in range(1, nrow):
        r = at(step, 0)[0]
        copy(slots_r.at[r], slots_r.at[r], sem1_s.at[step], sem1_r.at[r], at(step, 0)).wait_recv()
    total = slots_r[0]
    for q in range(1, nrow):
        total = total + slots_r[q]
    if part_m.shape[0] > chunk:
        total = jnp.concatenate([total, jnp.zeros((part_m.shape[0] - chunk, 128), F32)], axis=0)
    part_m[...] = total.astype(BF)
    col_copies = []
    for step in range(1, pairs):
        col_copies.append(copy(part_m, slots_m.at[pair], sem2_s.at[step], sem2_r.at[pair], along(step)))
        col_copies[-1].start()
    slots_m[pair] = part_m[...]

    lax.fori_loop(2, WINDOWS, feature_grads, 0)
    inv = 1.0 / group_size
    lg_ref[...] = (lacc[...] * inv).reshape(rows, cols, channels).astype(BF)
    for h in range(rows):
        racc0[h, 4:156] += racc4[h, 0:152]
        back_send[h] = racc0[h, 0:96].astype(BF)
    back_copies = [
        copy(back_send.at[:, 32:96], back_recv.at[:, 0:64], sem_bs.at[0], sem_br.at[0], at(0, -1)),
        copy(back_send.at[:, 0:32], back_recv.at[:, 64:96], sem_bs.at[1], sem_br.at[1], at(0, -2)),
    ]
    for c in back_copies:
        c.start()

    for c in vol_copies:
        c.wait_recv()
    clear_outside(vs, halo_v)
    write_shifts(vs, halo_v)

    def forward(k, carry):
        taps = []
        for b in range(3):
            for e in range(3):
                taps.append(vs[e, k, b : b + rows].reshape(cells, LANES))
        obuf[k] = dot(jnp.concatenate(taps, axis=1), band_n[...])
        return carry

    lax.fori_loop(0, 1, forward, 0)

    for step in range(1, pairs):
        p = lax.rem(pair + step, pairs)
        copy(part_m, slots_m.at[p], sem2_s.at[step], sem2_r.at[p], along(step)).wait_recv()
    total = slots_m[0].astype(F32)
    for q in range(1, pairs):
        total = total + slots_m[q].astype(F32)
    gathered[core, row] = (total * scale).astype(BF)
    gather_copies = []
    mine = gathered.at[core, row]
    for step in range(nrow):
        if step:
            gather_copies.append(copy(mine, mine, sem3_s.at[0, step], sem3_r.at[core, row], at(step, 0)))
        gather_copies.append(copy(mine, mine, sem3_s.at[1, step], sem3_r.at[core, row], at_mate(step)))
    for c in gather_copies:
        c.start()

    lax.fori_loop(1, WINDOWS, forward, 0)

    for h in range(rows):
        part = [obuf[k, cols * h : cols * (h + 1)].T for k in range(WINDOWS)]
        for k in range(WINDOWS):
            for i in range(OUT_D):
                j = i + 1
                value = part[k][feats * j : feats * (j + 1)]
                if i == 0 and k > 0:
                    value = value + part[k - 1][feats * (IN_D - 1) : feats * IN_D]
                if i == OUT_D - 1 and k < WINDOWS - 1:
                    value = value + part[k + 1][0:feats]
                cost_ref[OUT_D * k + i, h] = value.astype(BF)

    for c in back_copies:
        c.wait_recv()
    for h in range(rows):
        own = racc0[h, 96:160] + jnp.where(col < ncol - 1, back_recv[h, 0:64].astype(F32), 0.0)
        last = own[32:64] + jnp.where(col < ncol - 2, back_recv[h, 64:96].astype(F32), 0.0)
        rg_ref[h, 0:32] = (own[0:32] * inv).astype(BF)
        rg_ref[h, 32:64] = (last * inv).astype(BF)

    for step in range(nrow):
        r = lax.rem(row + step, nrow)
        if step:
            theirs = gathered.at[core, r]
            copy(theirs, theirs, sem3_s.at[0, step], sem3_r.at[core, r], at(step, 0)).wait_recv()
        theirs = gathered.at[1 - core, r]
        copy(theirs, theirs, sem3_s.at[1, step], sem3_r.at[1 - core, r], at_mate(step)).wait_recv()
    for side in range(2):
        for r in range(nrow):
            start = side * halfrows + r * chunk
            full[start : start + chunk] = gathered[side, r].astype(F32)[0:chunk]
    for b in range(3):
        for e in range(3):
            block = full[groups * (3 * b + e) : groups * (3 * b + e + 1)].T
            for a in range(3):
                wg_ref[a, b, e] = block[feats * (2 - a) : feats * (3 - a)]


    @pl.when(core == 0)
    def _():
        beyond.wait_send()
        forward_near.wait_send()

    sent = [near, middle, pair_copy] + cot_copies + vol_copies + back_copies
    for c in sent + row_copies + col_copies + gather_copies:
        c.wait_send()


def on_device(nrow, ncol, left, right, weight, cotangent):
    rows, cols, channels = left.shape
    groups, feats = weight.shape[3:]
    cells = rows * cols
    halfrows = -(-9 * groups // (16 * nrow)) * 8 * nrow
    chunk = halfrows // nrow
    slab = -(-chunk // 16) * 16
    scale = 1.0 / math.sqrt(DISP * rows * nrow * cols * ncol)
    dma = pltpu.SemaphoreType.DMA
    body = pltpu.VMEM((3, WINDOWS, rows + 2, cols, LANES), BF)
    edge = pltpu.VMEM((2, 16, LANES), BF)
    halo = pltpu.VMEM((2, 3, 16, LANES), BF)
    line = pltpu.VMEM((2, cols, DISP * feats), BF)
    outs = (
        jax.ShapeDtypeStruct((DISP, rows, feats, cols), BF),
        jax.ShapeDtypeStruct((3, 3, 3, feats, groups), F32),
        jax.ShapeDtypeStruct(left.shape, BF),
        jax.ShapeDtypeStruct(right.shape, BF),
    )
    args = (left, right, jnp.swapaxes(weight, 3, 4), jnp.swapaxes(cotangent, 2, 3))
    scratch = [pltpu.VMEM(a.shape, a.dtype) for a in args] + [
        pltpu.VMEM((rows, 96, channels), BF),
        pltpu.VMEM((rows, 160, channels), F32),
        pltpu.VMEM((rows, 160, channels), F32),
        pltpu.VMEM((rows, cols, channels), F32),
        pltpu.VMEM((OUT_D, channels, LANES), BF),
        pltpu.VMEM((9 * LANES, LANES), BF),
        pltpu.VMEM((9 * LANES, LANES), BF),
        body, body,
        pltpu.VMEM((LANES, WINDOWS * cells), BF),
        edge, edge, halo, halo, line, line,
        pltpu.VMEM((WINDOWS, cells, LANES), BF),
        pltpu.VMEM((2, cells, channels), F32),
        pltpu.VMEM((rows, 160, channels), F32),
        pltpu.VMEM((rows, 160, channels), F32),
        pltpu.VMEM((rows, 96, channels), BF),
        pltpu.VMEM((rows, 96, channels), BF),
        pltpu.VMEM((2 * halfrows, 128), F32),
        pltpu.VMEM((halfrows, 128), F32),
        pltpu.VMEM((halfrows, 128), F32),
        pltpu.VMEM((nrow, chunk, 128), F32),
        pltpu.VMEM((slab, 128), BF),
        pltpu.VMEM((ncol // 2, slab, 128), BF),
        pltpu.VMEM((2, nrow, slab, 128), BF),
        pltpu.VMEM((2 * halfrows, 128), F32),
        pltpu.VMEM((WINDOWS, cells, LANES), F32),
        dma((4,)), dma((4,)), dma((3,)), dma((8,)), dma((8,)), dma((8,)), dma((8,)),
        dma((2,)), dma((2,)), dma((2,)),
        dma((nrow,)), dma((nrow,)), dma((ncol // 2,)), dma((ncol // 2,)), dma((2, nrow)), dma((2, nrow)),
    ]
    anywhere = pl.BlockSpec(memory_space=pl.ANY)
    vmem = pl.BlockSpec(memory_space=pltpu.VMEM)
    results = pl.pallas_call(
        functools.partial(kernel, nrow, ncol, scale),
        out_shape=tuple(pltpu.VMEM(a.shape, a.dtype) for a in outs),
        in_specs=[anywhere] * 4,
        out_specs=(vmem,) * 4,
        scratch_shapes=scratch,
        compiler_params=pltpu.CompilerParams(
            collective_id=0, has_side_effects=True, vmem_limit_bytes=56 * 1024 * 1024
        ),
        name="cost_volume",
    )(*args)
    cost, weight_grad, left_grad, right_grad = results
    return jnp.swapaxes(cost, 2, 3), jnp.swapaxes(weight_grad, 3, 4), left_grad, right_grad


def solution(mesh):
    in_specs = (P("row", "col", None), P("row", "col", None), P(), P(None, "row", "col", None))
    out_specs = (P(None, "row", "col", None), P(), P("row", "col", None), P("row", "col", None))
    return jax.shard_map(
        functools.partial(on_device, mesh.shape["row"], mesh.shape["col"]),
        mesh=mesh, in_specs=in_specs, out_specs=out_specs, check_vma=False,
    )
```
